256 devices in a mesh: ctx: 64 (over y_lo, z, x), dp: 4 (over y_hi, core).
Axes of the slice: x: 4, y: 4 (y_hi: 2, y_lo: 2; y = y_hi * 2 + y_lo), z: 8, core: 2. Of those that a mesh axis runs over, the one named last changes fastest.
Arguments:
- frames_fwd: int32 [16384], P('ctx'), may hold values from 0 to 1023, never falling along the last dimension, each value on 1 to 64 neighbouring positions
- query_fwd: bfloat16 [16384, 2048], P('ctx', 'dp'), may hold values from -20 to 20
- keys_fwd: bfloat16 [16384, 2048], P('ctx', 'dp'), may hold values from -20 to 20
- values_fwd: bfloat16 [16384, 2048], P('ctx', 'dp'), may hold values from -6 to 6
- frames_bwd: int32 [16384], P('ctx'), may hold values from 0 to 1023, never falling along the last dimension, each value on 1 to 64 neighbouring positions
- query_bwd: bfloat16 [16384, 2048], P('ctx', 'dp'), may hold values from -6 to 6
- keys_bwd: bfloat16 [16384, 2048], P('ctx', 'dp'), may hold values from -6 to 6
- values_bwd: bfloat16 [16384, 2048], P('ctx', 'dp'), may hold values from -6 to 6
- attn_bwd: bfloat16 [16384, 2048], P('ctx', 'dp'), may hold values from -4 to 4
- logsumexp_bwd: float32 [16, 16384], P('dp', 'ctx'), may hold values from 4 to 6.5
- cotangent: bfloat16 [16384, 2048], P('ctx', 'dp'), may hold values from -6 to 6
- out_weight: bfloat16 [2048, 2048], P('dp'), may hold values from -0.125 to 0.125
Outputs:
- attended: bfloat16 [16384, 2048], P('ctx', 'dp')
- attended_logsumexp: float32 [16, 16384], P('dp', 'ctx')
- grad_query: float32 [16384, 2048], P('ctx', 'dp')
- grad_keys: float32 [16384, 2048], P('ctx', 'dp')
- grad_values: float32 [16384, 2048], P('ctx', 'dp')
- grad_weight: bfloat16 [2048, 2048], P('dp')
The draws below stay inside these ranges and needn't reach their ends.
Inputs may be any that keep to these rules, and one draw needn't show every extreme that they name: `frames_fwd`: frame ids never fall along the sequence; each frame spans 1 to 64 consecutive tokens and one spans exactly 64. `frames_bwd`: frame ids never fall along the sequence; each frame spans 1 to 64 consecutive tokens and one spans exactly 64.
All inputs are finite; a program needn't handle non-finite values.
Results may differ from the reference program's by a relative error of at most 0.0087.
Values may be sent and summed in bfloat16 or wider, within the bound.
No kernel may reach another device: no remote copies, remote signals or barrier semaphores. Data moves between devices by JAX's collectives and lax.ppermute only.
A program may use at most 64 MiB of HBM per device.

```python
import math
import jax
import jax.numpy as jnp
import numpy as np
from jax import lax

TOK_DEV = 256
HEADS = 16
HDIM = 128
DCOL = 2048
REACH = 4
FRAME_MOST = 64
HF = 2048
TOKENS = 16384
FRAMES = 1024
N_CTX = 64


def draw_query_fwd(key, part):
    key = jax.random.fold_in(key, 11)
    drawn = jnp.clip(jax.random.normal(key, (TOKENS, HF), jnp.float32), -6.0, 6.0)
    return drawn.astype(jnp.bfloat16)


def draw_keys_fwd(key, part):
    key = jax.random.fold_in(key, 12)
    drawn = jnp.clip(jax.random.normal(key, (TOKENS, HF), jnp.float32), -6.0, 6.0)
    return drawn.astype(jnp.bfloat16)


def shard_levels(key, shape, split, low, top_value):
    gain, own = 1.0, jax.random.fold_in(key, 6)
    for position, parts in split:
        steps = jnp.exp(jax.random.uniform(jax.random.fold_in(own, position), (parts,), jnp.float32, low / len(split), top_value / len(split)))
        gain = gain * jnp.repeat(steps, shape[position] // parts).reshape([-1 if axis == position else 1 for axis in range(len(shape))])
    return gain


def profile(count, total, most, slope):
    loads = [(1 << 20) // math.isqrt(grade ** slope) + 1 for grade in range(2, count + 1)]
    spare, counts = total - most - (count - 1), [1] * (count - 1)
    while spare > 0:
        free = [i for i in range(count - 1) if counts[i] < most]
        mass, left = sum([loads[i] for i in free]), spare
        for i in free:
            more = min(most - counts[i], max(1, left * loads[i] // mass), spare)
            counts[i] = counts[i] + more
            spare = spare - more
    return np.array([most] + counts)


def uneven(stream_key, count, total, most, slope):
    if count == 2:
        one = jax.random.randint(stream_key, (), max(1, total - most), min(most, total - 1) + 1)
        return jnp.stack([one, total - one])
    sizes = jnp.asarray(profile(count, total, most, slope), jnp.int32)
    pairs = (count - 1) // 2
    source_of, sink = sizes[1:1 + 2 * pairs:2], sizes[2:2 + 2 * pairs:2]
    slack = jnp.minimum(source_of - 1, most - sink)
    shifted = jax.random.randint(jax.random.fold_in(stream_key, 1), (pairs,), 0, 1 << 20) % (slack + 1)
    sizes = sizes.at[1:1 + 2 * pairs:2].set(source_of - shifted).at[2:2 + 2 * pairs:2].set(sink + shifted)
    return sizes[jax.random.permutation(jax.random.fold_in(stream_key, 2), count)]


def scatter_about(own_key, extent, width, bound, split=(), kind=jnp.bfloat16):
    values = width * jax.random.normal(own_key, extent, jnp.float32)
    if split:
        values = values * shard_levels(own_key, extent, split, -0.22, 0.18)
    return jnp.clip(values, -bound, bound).astype(kind)


def setup_inputs(seed: int = 0) -> dict:
    splits = jax.random.split(jax.random.key(seed), 13)
    frames_fwd = jnp.searchsorted(jnp.cumsum(uneven(splits[0], FRAMES, TOKENS, FRAME_MOST, 0)), jnp.arange(TOKENS), side="right").astype(jnp.int32)
    query_fwd = draw_query_fwd(jax.random.fold_in(splits[12], 71), 0)
    keys_fwd = draw_keys_fwd(jax.random.fold_in(splits[12], 71), 0)
    values_fwd = scatter_about(splits[3], (TOKENS, HF), 1.0, 6.0, ((0, 64), (1, 4)))
    frames_bwd = jnp.searchsorted(jnp.cumsum(uneven(splits[4], FRAMES, TOKENS, FRAME_MOST, 0)), jnp.arange(TOKENS), side="right").astype(jnp.int32)
    query_bwd = scatter_about(splits[5], (TOKENS, HF), 1.0, 6.0, ((0, 64), (1, 4)))
    keys_bwd = scatter_about(splits[6], (TOKENS, HF), 1.0, 6.0, ((0, 64), (1, 4)))
    values_bwd = scatter_about(splits[7], (TOKENS, HF), 1.0, 6.0, ((0, 64), (1, 4)))
    attn_bwd = scatter_about(splits[8], (TOKENS, HF), 0.3, 4.0, ((0, 64), (1, 4)))
    logsumexp_bwd = jnp.clip(4.0 + 2.5 * jax.random.uniform(splits[9], (HEADS, TOKENS), jnp.float32) ** shard_levels(splits[9], (HEADS, TOKENS), ((0, 4), (1, 64)), -0.2, 0.2), 4.0, 6.5)
    cotangent = scatter_about(splits[10], (TOKENS, DCOL), 1.0, 6.0, ((0, 64), (1, 4)))
    out_weight = scatter_about(splits[11], (HF, DCOL), HF ** -0.5, 0.125, ((0, 4),))
    return dict(frames_fwd=frames_fwd, query_fwd=query_fwd, keys_fwd=keys_fwd, values_fwd=values_fwd, frames_bwd=frames_bwd, query_bwd=query_bwd, keys_bwd=keys_bwd, values_bwd=values_bwd, attn_bwd=attn_bwd, logsumexp_bwd=logsumexp_bwd, cotangent=cotangent, out_weight=out_weight)


def head_split(matrix):
    return matrix.reshape(matrix.shape[0], HEADS, HDIM).astype(jnp.float32)

def round_bf16(values):
    return lax.optimization_barrier(values.astype(jnp.bfloat16)).astype(jnp.float32)

def forward_row(queries, key_rows, values, frames):
    softmax_scale = 1.0 / math.sqrt(HDIM)
    lead_rows = (REACH - 1) * TOK_DEV
    keys_pad = jnp.pad(key_rows, ((lead_rows, 0), (0, 0)))
    values_pad = jnp.pad(values, ((lead_rows, 0), (0, 0)))
    frames_pad = jnp.pad(frames, (lead_rows, 0))

    def one_block(block_index):
        row_start = (block_index * TOK_DEV).astype(jnp.int32)
        query_block = lax.dynamic_slice_in_dim(queries, row_start, TOK_DEV, 0)
        frame_query = lax.dynamic_slice_in_dim(frames, row_start, TOK_DEV, 0)
        key_window = lax.dynamic_slice_in_dim(keys_pad, row_start, REACH * TOK_DEV, 0)
        value_window = lax.dynamic_slice_in_dim(values_pad, row_start, REACH * TOK_DEV, 0)
        frame_keys = lax.dynamic_slice_in_dim(frames_pad, row_start, REACH * TOK_DEV, 0)
        positions = row_start - lead_rows + jnp.arange(REACH * TOK_DEV, dtype=jnp.int32)
        visible = (positions >= 0)[None, :] & (frame_keys[None, :] <= frame_query[:, None])
        scores = jnp.einsum('qhd,khd->hqk', head_split(query_block), head_split(key_window)) * softmax_scale
        scores = jnp.where(visible[None], scores, -jnp.inf)
        row_max = scores.max(-1)
        weights = jnp.exp(scores - row_max[:, :, None])
        row_sum = weights.sum(-1)
        summed = jnp.einsum('hqk,khd->qhd', round_bf16(weights), head_split(value_window))
        result = summed / row_sum.T[:, :, None]
        return (result.reshape(TOK_DEV, HF).astype(jnp.bfloat16), row_max + jnp.log(row_sum))
    attended, log_total = lax.map(one_block, jnp.arange(N_CTX, dtype=jnp.int32))
    return (attended.reshape(TOKENS, HF), log_total.transpose(1, 0, 2).reshape(HEADS, TOKENS))

def query_side(queries, key_rows, values, log_total, row_delta, grad_attn, frames):
    softmax_scale = 1.0 / math.sqrt(HDIM)
    lead_rows = (REACH - 1) * TOK_DEV
    keys_pad = jnp.pad(key_rows, ((lead_rows, 0), (0, 0)))
    values_pad = jnp.pad(values, ((lead_rows, 0), (0, 0)))
    frames_pad = jnp.pad(frames, (lead_rows, 0))

    def one_block(block_index):
        row_start = (block_index * TOK_DEV).astype(jnp.int32)
        query_block = lax.dynamic_slice_in_dim(queries, row_start, TOK_DEV, 0)
        grad_block = lax.dynamic_slice_in_dim(grad_attn, row_start, TOK_DEV, 0)
        frame_query = lax.dynamic_slice_in_dim(frames, row_start, TOK_DEV, 0)
        log_block = lax.dynamic_slice_in_dim(log_total, row_start, TOK_DEV, 1)
        delta_block = lax.dynamic_slice_in_dim(row_delta, row_start, TOK_DEV, 1)
        key_window = lax.dynamic_slice_in_dim(keys_pad, row_start, REACH * TOK_DEV, 0)
        value_window = lax.dynamic_slice_in_dim(values_pad, row_start, REACH * TOK_DEV, 0)
        frame_keys = lax.dynamic_slice_in_dim(frames_pad, row_start, REACH * TOK_DEV, 0)
        positions = row_start - lead_rows + jnp.arange(REACH * TOK_DEV, dtype=jnp.int32)
        visible = (positions >= 0)[None, :] & (frame_keys[None, :] <= frame_query[:, None])
        scores = jnp.einsum('qhd,khd->hqk', head_split(query_block), head_split(key_window)) * softmax_scale
        weights = jnp.where(visible[None], jnp.exp(scores - log_block[:, :, None]), 0.0)
        grad_weights = jnp.einsum('qhd,khd->hqk', head_split(grad_block), head_split(value_window))
        grad_scores = round_bf16(weights * (grad_weights - delta_block[:, :, None]))
        result = jnp.einsum('hqk,khd->qhd', grad_scores, head_split(key_window)) * softmax_scale
        return result.reshape(TOK_DEV, HF)
    return lax.map(one_block, jnp.arange(N_CTX, dtype=jnp.int32)).reshape(TOKENS, HF)

def key_side(queries, key_rows, values, log_total, row_delta, grad_attn, frames):
    softmax_scale = 1.0 / math.sqrt(HDIM)
    tail_rows = (REACH - 1) * TOK_DEV
    queries_pad = jnp.pad(queries, ((0, tail_rows), (0, 0)))
    grads_pad = jnp.pad(grad_attn, ((0, tail_rows), (0, 0)))
    frames_pad = jnp.pad(frames, (0, tail_rows))
    log_pad = jnp.pad(log_total, ((0, 0), (0, tail_rows)))
    delta_pad = jnp.pad(row_delta, ((0, 0), (0, tail_rows)))

    def one_block(block_index):
        row_start = (block_index * TOK_DEV).astype(jnp.int32)
        key_block = lax.dynamic_slice_in_dim(key_rows, row_start, TOK_DEV, 0)
        value_block = lax.dynamic_slice_in_dim(values, row_start, TOK_DEV, 0)
        frame_keys = lax.dynamic_slice_in_dim(frames, row_start, TOK_DEV, 0)
        query_window = lax.dynamic_slice_in_dim(queries_pad, row_start, REACH * TOK_DEV, 0)
        grad_window = lax.dynamic_slice_in_dim(grads_pad, row_start, REACH * TOK_DEV, 0)
        frame_query = lax.dynamic_slice_in_dim(frames_pad, row_start, REACH * TOK_DEV, 0)
        log_window = lax.dynamic_slice_in_dim(log_pad, row_start, REACH * TOK_DEV, 1)
        delta_window = lax.dynamic_slice_in_dim(delta_pad, row_start, REACH * TOK_DEV, 1)
        positions = row_start + jnp.arange(REACH * TOK_DEV, dtype=jnp.int32)
        visible = (positions < TOKENS)[:, None] & (frame_keys[None, :] <= frame_query[:, None])
        scores = jnp.einsum('qhd,khd->hqk', head_split(query_window), head_split(key_block)) * softmax_scale
        weights = jnp.where(visible[None], jnp.exp(scores - log_window[:, :, None]), 0.0)
        grad_values = jnp.einsum('hqk,qhd->khd', round_bf16(weights), head_split(grad_window))
        grad_weights = jnp.einsum('qhd,khd->hqk', head_split(grad_window), head_split(value_block))
        grad_scores = round_bf16(weights * (grad_weights - delta_window[:, :, None]))
        grad_keys = jnp.einsum('hqk,qhd->khd', grad_scores, head_split(query_window)) * softmax_scale
        return (grad_keys.reshape(TOK_DEV, HF), grad_values.reshape(TOK_DEV, HF))
    grad_keys, grad_values = lax.map(one_block, jnp.arange(N_CTX, dtype=jnp.int32))
    grad_keys = jnp.roll(grad_keys, REACH - 1, axis=0).reshape(TOKENS, HF)
    grad_values = jnp.roll(grad_values, REACH - 1, axis=0).reshape(TOKENS, HF)
    return (grad_keys, grad_values)

def reference(frames_fwd, query_fwd, keys_fwd, values_fwd, frames_bwd, query_bwd, keys_bwd, values_bwd, attn_bwd, logsumexp_bwd, cotangent, out_weight):
    attended, log_total = forward_row(query_fwd, keys_fwd, values_fwd, frames_fwd)
    grad_attn = jnp.dot(cotangent, out_weight.T, preferred_element_type=jnp.float32).astype(jnp.bfloat16)
    row_delta = lax.optimization_barrier(jnp.sum((grad_attn.astype(jnp.float32) * attn_bwd.astype(jnp.float32)).reshape(TOKENS, HEADS, HDIM), -1)).T
    grad_query = query_side(query_bwd, keys_bwd, values_bwd, logsumexp_bwd, row_delta, grad_attn, frames_bwd)
    grad_keys, grad_values = key_side(query_bwd, keys_bwd, values_bwd, logsumexp_bwd, row_delta, grad_attn, frames_bwd)
    grad_weight = jnp.dot(attn_bwd.T, cotangent, preferred_element_type=jnp.float32).astype(jnp.bfloat16)
    return (attended, log_total, grad_query, grad_keys, grad_values, grad_weight)
```

```python
import math

import jax
import jax.numpy as jnp
from jax import lax
from jax.experimental import pallas as pl
from jax.experimental.pallas import tpu as pltpu
from jax.sharding import Mesh
from jax.sharding import PartitionSpec as P

HDIM = 128
TOK = 256
REACH = 4
HALO = REACH - 1
SCALE = 1.0 / math.sqrt(HDIM)
LOG2E = math.log2(math.e)
LN2 = math.log(2.0)
FAR = 1e30
EXTRA = 16
VMEM_BYTES = 48 * 1024 * 1024

f32 = jnp.float32
bf16 = jnp.bfloat16

Q_F, K_F, V_F, K_B, V_B, Q_B, EXT = (TOK * i for i in range(7))
BLOCK_ROWS = EXT + EXTRA
HALO_FROM = K_F
GRAD_ROWS = TOK + EXTRA


def nt(a, b):
    return lax.dot_general(a, b, (((1,), (1,)), ((), ())), preferred_element_type=f32)


def nn(a, b):
    return lax.dot_general(a, b, (((1,), (0,)), ((), ())), preferred_element_type=f32)


def three_terms(value):
    high = value.astype(bf16).astype(f32)
    rest = value - high
    middle = rest.astype(bf16).astype(f32)
    return [high, middle, rest - middle]


def extra_rows(rows):
    halves = []
    for row in rows:
        halves += [row[:, :HDIM], row[:, HDIM:]]
    halves += [jnp.zeros((EXTRA - len(halves), HDIM), f32)]
    return jnp.concatenate(halves, axis=0).astype(bf16)


def row_of(extra, first, count=1):
    total = None
    for i in range(first, first + count):
        row = jnp.concatenate([extra[2 * i : 2 * i + 1], extra[2 * i + 1 : 2 * i + 2]], axis=1)
        total = row if total is None else total + row
    return total


def call(kernel, out_shape, n_smem, *args):
    spaces = [pltpu.SMEM] * n_smem + [pltpu.VMEM] * (len(args) - n_smem)
    single = not isinstance(out_shape, (tuple, list))
    out_space = pl.BlockSpec(memory_space=pltpu.VMEM)
    return pl.pallas_call(
        kernel,
        out_shape=out_shape,
        in_specs=[pl.BlockSpec(memory_space=space) for space in spaces],
        out_specs=out_space if single else [out_space] * len(out_shape),
        compiler_params=pltpu.CompilerParams(vmem_limit_bytes=VMEM_BYTES),
    )(*args)


def shape(*dims, dtype=bf16):
    return jax.ShapeDtypeStruct(dims, dtype)


def pack_kernel(qf, kf, vf, kb, vb, qb, lse, ends, out):
    for head in range(4):
        lanes = slice(head * HDIM, (head + 1) * HDIM)
        for i, ref in enumerate((qf, kf, vf, kb, vb, qb)):
            out[head, i * TOK : (i + 1) * TOK, :] = ref[:, lanes]
        rows = [ends[0:1, :], ends[1:2, :]] + three_terms(lse[head : head + 1, :])
        out[head, EXT:, :] = extra_rows(rows)


def part(own, halo, index, first, rows):
    if index < HALO:
        return halo[index, first - HALO_FROM : first - HALO_FROM + rows, :]
    return own[index - HALO, first : first + rows, :]


def forward_kernel(first_row, own, halo, out):
    off = jnp.where(first_row[0] == 0, FAR, 0.0).astype(f32)
    scale2 = SCALE * LOG2E
    key_index = lax.broadcasted_iota(jnp.int32, (TOK, TOK), 0)
    keys, values = [], []
    for i in range(7):
        keys.append(part(own, halo, i, K_F, TOK))
        values.append(part(own, halo, i, V_F, TOK).T)
    for a in range(4):
        query = own[a, Q_F : Q_F + TOK, :]
        ends = row_of(own[a, EXT:, :].astype(f32), 0).astype(jnp.int32)
        scores = []
        for b in range(a, a + REACH):
            s = nt(keys[b], query) * scale2
            if b < HALO:
                s = s - off
            if b == a + HALO:
                s = jnp.where(key_index <= ends, s, -FAR)
            scores.append(s)
        top = scores[0].max(0, keepdims=True)
        for s in scores[1:]:
            top = jnp.maximum(top, s.max(0, keepdims=True))
        total = jnp.zeros((1, TOK), f32)
        summed = jnp.zeros((HDIM, TOK), f32)
        for b, s in zip(range(a, a + REACH), scores):
            weights = jnp.exp2(s - top)
            total = total + weights.sum(0, keepdims=True)
            summed = summed + nn(values[b], weights.astype(bf16))
        out[a, :TOK, :] = (summed / total).T.astype(bf16)
        out[a, TOK:, :] = extra_rows(three_terms(top * LN2 + jnp.log(total)))


def backward_kernel(first_row, own, halo, grads, grads_halo, forward_out, out):
    off = jnp.where(first_row[0] == 0, FAR, 0.0).astype(f32)
    scale2 = SCALE * LOG2E
    key_index = lax.broadcasted_iota(jnp.int32, (TOK, TOK), 0)
    out[:, 3 * TOK :, :] = forward_out[...]

    def grad_rows(index, first, rows):
        if index < HALO:
            return grads_halo[index, first : first + rows, :]
        return grads[index - HALO, first : first + rows, :]

    extra = [part(own, halo, i, EXT, EXTRA).astype(f32) for i in range(7)]
    delta = [row_of(grad_rows(i, TOK, EXTRA).astype(f32), 0, 3) for i in range(7)]
    totals = [row_of(extra[i], 2, 3) * LOG2E for i in range(7)]
    grad_query = [None] * 7
    for b in range(7):
        key = part(own, halo, b, K_B, TOK)
        value = part(own, halo, b, V_B, TOK)
        key_turned = key.T
        grad_key = grad_value = None
        for a in range(b, min(b + REACH, 7)):
            if a < HALO and b > HALO:
                continue
            query = part(own, halo, a, Q_B, TOK)
            grad = grad_rows(a, 0, TOK)
            total = totals[a] + off if (a >= HALO and b < HALO) else totals[a]
            weights = jnp.exp2(nt(key, query) * scale2 - total)
            if a == b:
                ends = row_of(extra[a], 1).astype(jnp.int32)
                weights = jnp.where(key_index <= ends, weights, 0.0)
            scores = (weights * (nt(value, grad) - delta[a])).astype(bf16)
            if b <= HALO:
                dk, dv = nn(scores, query), nn(weights.astype(bf16), grad)
                grad_key = dk if grad_key is None else grad_key + dk
                grad_value = dv if grad_value is None else grad_value + dv
            if a >= HALO:
                dq = nn(key_turned, scores)
                grad_query[a] = dq if grad_query[a] is None else grad_query[a] + dq
        if b <= HALO:
            out[b, TOK : 2 * TOK, :] = (grad_key * SCALE).astype(bf16)
            out[b, 2 * TOK : 3 * TOK, :] = grad_value.astype(bf16)
    for a in range(4):
        out[a, :TOK, :] = (grad_query[a + HALO] * SCALE).T.astype(bf16)


def unpack_kernel(packed, attended, log_total, grad_query, grad_keys, grad_values):
    for head in range(4):
        lanes = slice(head * HDIM, (head + 1) * HDIM)
        grad_query[:, lanes] = packed[head, :TOK, :].astype(f32)
        grad_keys[:, lanes] = packed[head, TOK : 2 * TOK, :].astype(f32)
        grad_values[:, lanes] = packed[head, 2 * TOK : 3 * TOK, :].astype(f32)
        attended[:, lanes] = packed[head, 3 * TOK : 4 * TOK, :]
        extra = packed[head, 4 * TOK :, :].astype(f32)
        log_total[head : head + 1, :] = row_of(extra, 0, 3)


def grad_kernel(place, c0, c1, c2, c3, o0, o1, o2, o3, weight, attn, attn_far, out):
    y_lo, y_hi, core = place[0], place[1], place[2]
    own = {(0, 0): c0, (0, 1): o0, (1, 0): c2, (1, 1): o2}
    far = {(0, 0): (c1, c3), (0, 1): (o1, o3), (1, 0): (c3, c1), (1, 1): (o3, o1)}
    width = 4 * HDIM
    half = attn[:, pl.ds(pl.multiple_of(y_lo * TOK, TOK), TOK)].T
    half_far = attn_far[...].T
    total = None
    for (hi, side), cot_ref in own.items():
        y = y_hi + hi - 2 * y_hi * hi
        c = core + side - 2 * core * side
        group = 2 * y + c
        cot = cot_ref[...]
        term = nt(cot, weight[:, pl.ds(pl.multiple_of(group * width, width), width)])
        total = term if total is None else total + term
        pair = far[hi, side]
        cot_far = jnp.where(y_lo == 1, pair[0][...], pair[1][...])
        product = (nn(half, cot) + nn(half_far, cot_far)).astype(bf16)
        for j in range(4):
            rows = pl.ds(GRAD_ROWS + j * TOK, TOK)
            out[group, rows, :] = product[:, j * HDIM : (j + 1) * HDIM]
    grad = total.astype(bf16)
    for head in range(4):
        lanes = slice(head * HDIM, (head + 1) * HDIM)
        product = grad[:, lanes].astype(f32) * attn[:, lanes].astype(f32)
        out[head, :TOK, :] = grad[:, lanes]
        out[head, TOK:GRAD_ROWS, :] = extra_rows(three_terms(product.T.sum(0, keepdims=True)))


def sum_kernel(parts, out):
    total = parts[0, GRAD_ROWS:, :].astype(f32)
    for i in range(1, 4):
        total = total + parts[i, GRAD_ROWS:, :].astype(f32)
    out[...] = total.astype(bf16)


def last_sum_kernel(parts, out):
    total = parts[0].astype(f32)
    for i in range(1, 8):
        total = total + parts[i].astype(f32)
    total = total.astype(bf16)
    for i in range(8):
        out[i] = total


def assemble_kernel(parts, out):
    for y in range(2):
        for x in range(4):
            for j in range(4):
                lanes = slice((x * 4 + j) * HDIM, (x * 4 + j + 1) * HDIM)
                out[y * TOK : (y + 1) * TOK, lanes] = parts[y * 4 + x, j * TOK : (j + 1) * TOK, :]


def across(value, axes):
    return lax.all_to_all(value, axes, 0, 0, tiled=True)


def along_y(value, distance):
    def place(y):
        return (y % 2) * 2 + (y // 2) % 2

    return lax.ppermute(value, ("yl", "yh"), [(place(y), place((y + distance) % 4)) for y in range(4)])


def next_row(value):
    return lax.ppermute(value, ("yl", "z"), [(i, (i + 1) % 16) for i in range(16)])


def other(value, axis):
    return lax.ppermute(value, axis, [(0, 1), (1, 0)])


def block_ends(frames):
    return (frames[:, None] <= frames[None, :]).astype(f32).sum(0) - 1.0


def body(
    frames_fwd,
    query_fwd,
    keys_fwd,
    values_fwd,
    frames_bwd,
    query_bwd,
    keys_bwd,
    values_bwd,
    attn_bwd,
    logsumexp_bwd,
    cotangent,
    out_weight,
):
    y_lo = lax.axis_index("yl")
    place = jnp.stack([y_lo, lax.axis_index("yh"), lax.axis_index("core")]).astype(jnp.int32)
    row = (lax.axis_index(("yl", "z"))).astype(jnp.int32).reshape(1)

    cots = [cotangent] + [along_y(cotangent, d) for d in range(1, 4)]
    attn_far = other(lax.dynamic_slice_in_dim(attn_bwd, (1 - y_lo) * TOK, TOK, 1), "yl")

    ends = jnp.stack([block_ends(frames_fwd), block_ends(frames_bwd)])
    packed = call(
        pack_kernel,
        shape(4, BLOCK_ROWS, HDIM),
        0,
        query_fwd,
        keys_fwd,
        values_fwd,
        keys_bwd,
        values_bwd,
        query_bwd,
        logsumexp_bwd,
        ends,
    )
    own = across(packed, "x")
    halo = next_row(own[1:, HALO_FROM:, :])

    others = [other(c, "core") for c in cots]
    grads_packed = call(
        grad_kernel,
        shape(4, GRAD_ROWS + 4 * TOK, HDIM),
        1,
        place,
        *cots,
        *others,
        out_weight,
        attn_bwd,
        attn_far,
    )
    grads = across(grads_packed, "x")
    grads_own = grads[:, :GRAD_ROWS, :]
    grads_halo = next_row(grads[1:, :GRAD_ROWS, :])

    summed = call(sum_kernel, shape(4 * TOK, HDIM), 0, grads)
    parts = across(summed.reshape(8, HDIM, HDIM), "z")
    chunks = call(last_sum_kernel, shape(8, HDIM, HDIM), 0, parts)
    gathered = across(chunks, "z").reshape(1, 4 * TOK, HDIM)

    forward_out = call(forward_kernel, shape(4, GRAD_ROWS, HDIM), 1, row, own, halo)
    backward_out = call(
        backward_kernel,
        shape(4, 4 * TOK + EXTRA, HDIM),
        1,
        row,
        own,
        halo,
        grads_own,
        grads_halo,
        forward_out,
    )
    back = across(backward_out, "x")
    attended, log_total, grad_query, grad_keys, grad_values = call(
        unpack_kernel,
        [
            shape(TOK, 4 * HDIM),
            shape(4, TOK, dtype=f32),
            shape(TOK, 4 * HDIM, dtype=f32),
            shape(TOK, 4 * HDIM, dtype=f32),
            shape(TOK, 4 * HDIM, dtype=f32),
        ],
        0,
        back,
    )
    whole = across(jnp.broadcast_to(gathered, (8, 4 * TOK, HDIM)), ("yl", "x"))
    grad_weight = call(assemble_kernel, shape(2 * TOK, 16 * HDIM), 0, whole)
    return (attended, log_total, grad_query, grad_keys, grad_values, grad_weight)


def solution(mesh):
    fine = Mesh(mesh.devices.reshape(2, 8, 4, 2, 2), ("yl", "z", "x", "yh", "core"))
    ctx, dp = ("yl", "z", "x"), ("yh", "core")
    in_specs = (
        P(ctx),
        P(ctx, dp),
        P(ctx, dp),
        P(ctx, dp),
        P(ctx),
        P(ctx, dp),
        P(ctx, dp),
        P(ctx, dp),
        P(ctx, dp),
        P(dp, ctx),
        P(ctx, dp),
        P(dp, None),
    )
    out_specs = (
        P(ctx, dp),
        P(dp, ctx),
        P(ctx, dp),
        P(ctx, dp),
        P(ctx, dp),
        P(dp, None),
    )
    return jax.shard_map(body, mesh=fine, in_specs=in_specs, out_specs=out_specs, check_vma=False)
```

```python
import math

import jax
import jax.numpy as jnp
from jax import lax
from jax.experimental import pallas as pl
from jax.experimental.pallas import tpu as pltpu
from jax.sharding import Mesh
from jax.sharding import PartitionSpec as P

HDIM = 128
TOK = 256
REACH = 4
HALO = REACH - 1
SCALE = 1.0 / math.sqrt(HDIM)
LOG2E = math.log2(math.e)
LN2 = math.log(2.0)
FAR = 1e30
EXTRA = 16
VMEM_BYTES = 48 * 1024 * 1024

f32 = jnp.float32
bf16 = jnp.bfloat16

Q_F, K_F, V_F, K_B, V_B, Q_B, EXT = (TOK * i for i in range(7))
BLOCK_ROWS = EXT + EXTRA
HALO_FROM = K_F
GRAD_ROWS = TOK + EXTRA
BACK_ROWS = 4 * TOK + EXTRA


def nt(a, b):
    return lax.dot_general(a, b, (((1,), (1,)), ((), ())), preferred_element_type=f32)


def nn(a, b):
    return lax.dot_general(a, b, (((1,), (0,)), ((), ())), preferred_element_type=f32)


def three_terms(value):
    high = value.astype(bf16).astype(f32)
    rest = value - high
    middle = rest.astype(bf16).astype(f32)
    return [high, middle, rest - middle]


def extra_rows(rows):
    halves = []
    for row in rows:
        halves += [row[:, :HDIM], row[:, HDIM:]]
    halves += [jnp.zeros((EXTRA - len(halves), HDIM), f32)]
    return jnp.concatenate(halves, axis=0).astype(bf16)


def row_of(extra, first, count=1):
    total = None
    for i in range(first, first + count):
        row = jnp.concatenate([extra[2 * i : 2 * i + 1], extra[2 * i + 1 : 2 * i + 2]], axis=1)
        total = row if total is None else total + row
    return total


def in_hbm(value):
    return pltpu.with_memory_space_constraint(value, pltpu.HBM)


def call(kernel, out_shape, n_smem, *args, scratch=()):
    spaces = [pltpu.SMEM] * n_smem + [pltpu.VMEM] * (len(args) - n_smem)
    single = not isinstance(out_shape, (tuple, list))
    out_space = pl.BlockSpec(memory_space=pltpu.VMEM)
    return pl.pallas_call(
        kernel,
        out_shape=out_shape,
        in_specs=[pl.BlockSpec(memory_space=space) for space in spaces],
        scratch_shapes=scratch,
        out_specs=out_space if single else [out_space] * len(out_shape),
        compiler_params=pltpu.CompilerParams(vmem_limit_bytes=VMEM_BYTES),
    )(*args)


def shape(*dims, dtype=bf16):
    return jax.ShapeDtypeStruct(dims, dtype)


def block_ends(frames):
    across_lanes = jnp.broadcast_to(frames, (TOK, TOK))
    seen = jnp.where(across_lanes.T <= across_lanes, 1.0, 0.0)
    return seen.sum(0, keepdims=True) - 1.0


def pack_kernel(place, qf, kf, vf, kb, vb, qb, lse, attn, cot, frames_fwd, frames_bwd, out, to_pair):
    far_half = pl.multiple_of((1 - place[0]) * TOK, TOK)
    to_pair[:, : 4 * HDIM] = cot[...]
    to_pair[:, 4 * HDIM :] = attn[:, pl.ds(far_half, TOK)]
    ends = [block_ends(frames_fwd[...].astype(f32)), block_ends(frames_bwd[...].astype(f32))]
    for head in range(4):
        lanes = slice(head * HDIM, (head + 1) * HDIM)
        for i, ref in enumerate((qf, kf, vf, kb, vb, qb)):
            out[head, i * TOK : (i + 1) * TOK, :] = ref[:, lanes]
        rows = ends + three_terms(lse[head : head + 1, :])
        out[head, EXT:, :] = extra_rows(rows)


def part(own, halo, index, first, rows):
    if index < HALO:
        return halo[index, first - HALO_FROM : first - HALO_FROM + rows, :]
    return own[index - HALO, first : first + rows, :]


def forward_kernel(place, own, halo, out):
    off = jnp.where(place[0] == 0, FAR, 0.0).astype(f32)
    scale2 = SCALE * LOG2E
    key_index = lax.broadcasted_iota(jnp.int32, (TOK, TOK), 0)
    keys, values = [], []
    for i in range(7):
        keys.append(part(own, halo, i, K_F, TOK))
        values.append(part(own, halo, i, V_F, TOK).T)
    for a in range(4):
        query = own[a, Q_F : Q_F + TOK, :]
        ends = row_of(own[a, EXT:, :].astype(f32), 0).astype(jnp.int32)
        scores = []
        for b in range(a, a + REACH):
            s = nt(keys[b], query) * scale2
            if b < HALO:
                s = s - off
            if b == a + HALO:
                s = jnp.where(key_index <= ends, s, -FAR)
            scores.append(s)
        top = scores[0].max(0, keepdims=True)
        for s in scores[1:]:
            top = jnp.maximum(top, s.max(0, keepdims=True))
        total = jnp.zeros((1, TOK), f32)
        summed = jnp.zeros((HDIM, TOK), f32)
        for b, s in zip(range(a, a + REACH), scores):
            weights = jnp.exp2(s - top)
            total = total + weights.sum(0, keepdims=True)
            summed = summed + nn(values[b], weights.astype(bf16))
        out[a, :TOK, :] = (summed / total).T.astype(bf16)
        out[a, TOK:, :] = extra_rows(three_terms(top * LN2 + jnp.log(total)))


def backward_kernel(place, own, halo, grads, forward_out, rest, grad_kv, ahead):
    off = jnp.where(place[0] == 0, FAR, 0.0).astype(f32)
    scale2 = SCALE * LOG2E
    key_index = lax.broadcasted_iota(jnp.int32, (TOK, TOK), 0)
    rest[:, TOK:, :] = forward_out[...]

    extra = [own[i, EXT:, :].astype(f32) for i in range(4)]
    delta = [row_of(grads[i, TOK:GRAD_ROWS, :].astype(f32), 0, 3) for i in range(4)]
    totals = [row_of(extra[i], 2, 3) * LOG2E for i in range(4)]
    grad_query = [None] * 4
    for b in range(7):
        key = part(own, halo, b, K_B, TOK)
        value = part(own, halo, b, V_B, TOK)
        key_turned = key.T
        grad_key = grad_value = None
        for a in range(max(b - HALO, 0), min(b, HALO) + 1):
            query = own[a, Q_B : Q_B + TOK, :]
            grad = grads[a, :TOK, :]
            total = totals[a] + off if b < HALO else totals[a]
            weights = jnp.exp2(nt(key, query) * scale2 - total)
            if a + HALO == b:
                ends = row_of(extra[a], 1).astype(jnp.int32)
                weights = jnp.where(key_index <= ends, weights, 0.0)
            scores = (weights * (nt(value, grad) - delta[a])).astype(bf16)
            dk, dv = nn(scores, query), nn(weights.astype(bf16), grad)
            grad_key = dk if grad_key is None else grad_key + dk
            grad_value = dv if grad_value is None else grad_value + dv
            dq = nn(key_turned, scores)
            grad_query[a] = dq if grad_query[a] is None else grad_query[a] + dq
        if b <= HALO:
            grad_kv[b, :TOK, :] = grad_key * SCALE
            grad_kv[b, TOK:, :] = grad_value
        else:
            ahead[b - 4, :TOK, :] = (grad_key * SCALE).astype(bf16)
            ahead[b - 4, TOK:, :] = grad_value.astype(bf16)
    for a in range(4):
        rest[a, :TOK, :] = (grad_query[a] * SCALE).T.astype(bf16)


def finish_kernel(place, rest, grad_kv, behind, out0, out1, out2, out3, out):
    for b in range(4):
        total = grad_kv[b]
        if b < HALO:
            total = total + behind[b].astype(f32)
        out[b, : 2 * TOK, :] = total.astype(bf16)
        out[b, 2 * TOK :, :] = rest[b]
    for distance, ref in enumerate((out0, out1, out2, out3)):
        ref[...] = out[lax.rem(place[1] + distance, 4)]


def unpack_kernel(place, in0, in1, in2, in3, attended, log_total, grad_query, grad_keys, grad_values):
    for distance, ref in enumerate((in0, in1, in2, in3)):
        head = lax.rem(place[1] + 4 - distance, 4)
        lanes = pl.ds(pl.multiple_of(head * HDIM, HDIM), HDIM)
        grad_keys[:, lanes] = ref[:TOK, :].astype(f32)
        grad_values[:, lanes] = ref[TOK : 2 * TOK, :].astype(f32)
        grad_query[:, lanes] = ref[2 * TOK : 3 * TOK, :].astype(f32)
        attended[:, lanes] = ref[3 * TOK : 4 * TOK, :]
        extra = ref[4 * TOK :, :].astype(f32)
        log_total[pl.ds(head, 1), :] = row_of(extra, 0, 3)


def grad_kernel(place, c0, o0, c1, o1, c2, o2, c3, o3, weight, attn, out):
    y_lo, y_hi, core = place[0], place[1], place[2]
    width = 4 * HDIM
    half = attn[:, pl.ds(pl.multiple_of(y_lo * TOK, TOK), TOK)].T
    half_far = c1[:, width:].T
    total = None
    for hi, side, near, far in ((0, 0, c0, c1), (0, 1, o0, o1), (1, 0, c2, c3), (1, 1, o2, o3)):
        y = y_hi + hi - 2 * y_hi * hi
        c = core + side - 2 * core * side
        group = 2 * y + c
        cot = near[...]
        term = nt(cot, weight[:, pl.ds(pl.multiple_of(group * width, width), width)])
        total = term if total is None else total + term
        product = (nn(half, cot) + nn(half_far, far[:, :width])).astype(bf16)
        for j in range(4):
            rows = pl.ds(GRAD_ROWS + j * TOK, TOK)
            out[group, rows, :] = product[:, j * HDIM : (j + 1) * HDIM]
    grad = total.astype(bf16)
    for head in range(4):
        lanes = slice(head * HDIM, (head + 1) * HDIM)
        product = grad[:, lanes].astype(f32) * attn[:, lanes].astype(f32)
        out[head, :TOK, :] = grad[:, lanes]
        out[head, TOK:GRAD_ROWS, :] = extra_rows(three_terms(product.T.sum(0, keepdims=True)))


def sum_kernel(parts, out):
    total = parts[0, GRAD_ROWS:, :].astype(f32)
    for i in range(1, 4):
        total = total + parts[i, GRAD_ROWS:, :].astype(f32)
    out[...] = total.astype(bf16)


def last_sum_kernel(parts, out):
    total = parts[0].astype(f32)
    for i in range(1, 8):
        total = total + parts[i].astype(f32)
    total = total.astype(bf16)
    for i in range(8):
        out[i] = total


def assemble_kernel(place, *refs):
    out = refs[-1]
    for far in range(2):
        y = place[0] + far - 2 * place[0] * far
        rows = pl.ds(pl.multiple_of(y * TOK, TOK), TOK)
        for distance in range(4):
            x = lax.rem(place[1] + 4 - distance, 4)
            ref = refs[far * 4 + distance]
            for j in range(4):
                lanes = pl.ds(pl.multiple_of((x * 4 + j) * HDIM, HDIM), HDIM)
                out[rows, lanes] = ref[j * TOK : (j + 1) * TOK, :]


def across(value, axes):
    return lax.all_to_all(value, axes, 0, 0, tiled=True)


def diagonal(value):
    return lax.ppermute(value, ("yl", "yh"), [(0, 3), (1, 2), (2, 1), (3, 0)])


def along_x(value, distance):
    return lax.ppermute(value, "x", [(i, (i + distance) % 4) for i in range(4)])


def next_row(value):
    return lax.ppermute(value, ("yl", "z"), [(i, (i + 1) % 16) for i in range(16)])


def other(value, axis):
    return lax.ppermute(value, axis, [(0, 1), (1, 0)])


def body(
    frames_fwd,
    query_fwd,
    keys_fwd,
    values_fwd,
    frames_bwd,
    query_bwd,
    keys_bwd,
    values_bwd,
    attn_bwd,
    logsumexp_bwd,
    cotangent,
    out_weight,
):
    y_lo = lax.axis_index("yl")
    place = jnp.stack([y_lo, lax.axis_index("yh"), lax.axis_index("core")]).astype(jnp.int32)
    place_x = jnp.stack([lax.axis_index(("yl", "z")), lax.axis_index("x")]).astype(jnp.int32)

    packed, to_pair = call(
        pack_kernel,
        [pltpu.HBM((4, BLOCK_ROWS, HDIM), bf16), pltpu.HBM((TOK, 6 * HDIM), bf16)],
        1,
        place,
        *map(in_hbm, (query_fwd, keys_fwd, values_fwd, keys_bwd, values_bwd, query_bwd)),
        *map(in_hbm, (logsumexp_bwd, attn_bwd, cotangent)),
        in_hbm(frames_fwd.reshape(1, TOK)),
        in_hbm(frames_bwd.reshape(1, TOK)),
    )
    cots = [cotangent, other(to_pair, "yl"), other(cotangent, "yh"), diagonal(cotangent)]
    own = across(packed, "x")
    halo = next_row(own[1:, HALO_FROM:Q_B, :])

    pairs = [(c, other(c[:, : 4 * HDIM], "core")) for c in cots]
    grads_packed = call(
        grad_kernel,
        pltpu.HBM((4, GRAD_ROWS + 4 * TOK, HDIM), bf16),
        1,
        place,
        *sum(pairs, ()),
        in_hbm(out_weight),
        in_hbm(attn_bwd),
    )
    grads = across(grads_packed, "x")
    grads_own = grads[:, :GRAD_ROWS, :]

    summed = call(sum_kernel, shape(4 * TOK, HDIM), 0, grads)
    parts = across(summed.reshape(8, HDIM, HDIM), "z")
    forward_out = call(forward_kernel, shape(4, GRAD_ROWS, HDIM), 1, place_x, own, halo)
    parts, forward_out = lax.optimization_barrier((parts, forward_out))
    chunks = call(last_sum_kernel, pltpu.HBM((8, HDIM, HDIM), bf16), 0, parts)
    gathered = across(chunks, "z").reshape(4 * TOK, HDIM)
    rest, grad_kv, ahead = call(
        backward_kernel,
        [shape(4, TOK + GRAD_ROWS, HDIM), shape(4, 2 * TOK, HDIM, dtype=f32), pltpu.HBM((HALO, 2 * TOK, HDIM), bf16)],
        1,
        place_x,
        own,
        halo,
        grads_own,
        forward_out,
    )
    behind = next_row(ahead)
    gathered, ahead = lax.optimization_barrier((gathered, ahead))
    row_parts = [gathered] + [along_x(gathered, d) for d in range(1, 4)]
    far_parts = [other(part, "yl") for part in row_parts]
    behind, row_parts, far_parts[0] = lax.optimization_barrier((behind, row_parts, far_parts[0]))
    outs = call(
        finish_kernel,
        [pltpu.HBM((BACK_ROWS, HDIM), bf16)] * 4,
        1,
        place_x,
        rest,
        grad_kv,
        behind,
        scratch=[pltpu.VMEM((4, BACK_ROWS, HDIM), bf16)],
    )
    back = [outs[0]] + [along_x(outs[d], d) for d in range(1, 4)]
    attended, log_total, grad_query, grad_keys, grad_values = call(
        unpack_kernel,
        [
            shape(TOK, 4 * HDIM),
            shape(4, TOK, dtype=f32),
            shape(TOK, 4 * HDIM, dtype=f32),
            shape(TOK, 4 * HDIM, dtype=f32),
            shape(TOK, 4 * HDIM, dtype=f32),
        ],
        1,
        place_x,
        *back,
    )
    place_xy = jnp.stack([y_lo, lax.axis_index("x")]).astype(jnp.int32)
    grad_weight = call(assemble_kernel, shape(2 * TOK, 16 * HDIM), 1, place_xy, *row_parts, *far_parts)
    return (attended, log_total, grad_query, grad_keys, grad_values, grad_weight)


def solution(mesh):
    fine = Mesh(mesh.devices.reshape(2, 8, 4, 2, 2), ("yl", "z", "x", "yh", "core"))
    ctx, dp = ("yl", "z", "x"), ("yh", "core")
    in_specs = (
        P(ctx),
        P(ctx, dp),
        P(ctx, dp),
        P(ctx, dp),
        P(ctx),
        P(ctx, dp),
        P(ctx, dp),
        P(ctx, dp),
        P(ctx, dp),
        P(dp, ctx),
        P(ctx, dp),
        P(dp, None),
    )
    out_specs = (
        P(ctx, dp),
        P(dp, ctx),
        P(ctx, dp),
        P(ctx, dp),
        P(ctx, dp),
        P(dp, None),
    )
    return jax.shard_map(body, mesh=fine, in_specs=in_specs, out_specs=out_specs, check_vma=False)
```

```python
import math

import jax
import jax.numpy as jnp
from jax import lax
from jax.experimental import pallas as pl
from jax.experimental.pallas import tpu as pltpu
from jax.sharding import Mesh
from jax.sharding import PartitionSpec as P

HDIM = 128
TOK = 256
REACH = 4
HALO = REACH - 1
SCALE = 1.0 / math.sqrt(HDIM)
LOG2E = math.log2(math.e)
LN2 = math.log(2.0)
FAR = 1e30
EXTRA = 16
VMEM_BYTES = 48 * 1024 * 1024

f32 = jnp.float32
bf16 = jnp.bfloat16

Q_F, K_F, V_F, K_B, V_B, Q_B, EXT = (TOK * i for i in range(7))
BLOCK_ROWS = EXT + EXTRA
HALO_FROM = K_F
GRAD_ROWS = TOK + EXTRA
BACK_ROWS = 4 * TOK + EXTRA


def nt(a, b):
    return lax.dot_general(a, b, (((1,), (1,)), ((), ())), preferred_element_type=f32)


def nn(a, b):
    return lax.dot_general(a, b, (((1,), (0,)), ((), ())), preferred_element_type=f32)


def three_terms(value):
    high = value.astype(bf16).astype(f32)
    rest = value - high
    middle = rest.astype(bf16).astype(f32)
    return [high, middle, rest - middle]


def extra_rows(rows):
    halves = []
    for row in rows:
        halves += [row[:, :HDIM], row[:, HDIM:]]
    halves += [jnp.zeros((EXTRA - len(halves), HDIM), f32)]
    return jnp.concatenate(halves, axis=0).astype(bf16)


def row_of(extra, first, count=1):
    total = None
    for i in range(first, first + count):
        row = jnp.concatenate([extra[2 * i : 2 * i + 1], extra[2 * i + 1 : 2 * i + 2]], axis=1)
        total = row if total is None else total + row
    return total


def in_hbm(value):
    return pltpu.with_memory_space_constraint(value, pltpu.HBM)


def call(kernel, out_shape, n_smem, *args, scratch=(), raw_in=(), raw_out=False):
    spaces = [pltpu.SMEM] * n_smem + [pltpu.VMEM] * (len(args) - n_smem)
    for i in raw_in:
        spaces[i] = pltpu.HBM
    single = not isinstance(out_shape, (tuple, list))
    out_space = pl.BlockSpec(memory_space=pltpu.HBM if raw_out else pltpu.VMEM)
    return pl.pallas_call(
        kernel,
        out_shape=out_shape,
        in_specs=[pl.BlockSpec(memory_space=space) for space in spaces],
        scratch_shapes=scratch,
        out_specs=out_space if single else [out_space] * len(out_shape),
        compiler_params=pltpu.CompilerParams(vmem_limit_bytes=VMEM_BYTES),
    )(*args)


def shape(*dims, dtype=bf16):
    return jax.ShapeDtypeStruct(dims, dtype)


def block_ends(frames):
    across_lanes = jnp.broadcast_to(frames, (TOK, TOK))
    seen = jnp.where(across_lanes.T <= across_lanes, 1.0, 0.0)
    return seen.sum(0, keepdims=True) - 1.0


def pack_kernel(
    place, qf, kf, vf, kb, vb, qb, lse, attn, cot, frames_fwd, frames_bwd, out, to_pair, packed, paired, sems
):
    far_half = pl.multiple_of((1 - place[0]) * TOK, TOK)
    paired[:, : 4 * HDIM] = cot[...]
    paired[:, 4 * HDIM :] = attn[:, pl.ds(far_half, TOK)]
    copies = [pltpu.make_async_copy(paired, to_pair, sems.at[4])]
    copies[0].start()
    ends = [block_ends(frames_fwd[...].astype(f32)), block_ends(frames_bwd[...].astype(f32))]
    for head in range(4):
        lanes = slice(head * HDIM, (head + 1) * HDIM)
        for i, ref in enumerate((qf, kf, vf, kb, vb, qb)):
            packed[head, i * TOK : (i + 1) * TOK, :] = ref[:, lanes]
        rows = ends + three_terms(lse[head : head + 1, :])
        packed[head, EXT:, :] = extra_rows(rows)
        copy = pltpu.make_async_copy(packed.at[head], out.at[head], sems.at[head])
        copy.start()
        copies.append(copy)
    for copy in copies:
        copy.wait()


def part(own, halo, index, first, rows):
    if index < HALO:
        return halo[index, first - HALO_FROM : first - HALO_FROM + rows, :]
    return own[index - HALO, first : first + rows, :]


def forward_kernel(place, own, halo, out):
    off = jnp.where(place[0] == 0, FAR, 0.0).astype(f32)
    scale2 = SCALE * LOG2E
    key_index = lax.broadcasted_iota(jnp.int32, (TOK, TOK), 0)
    keys, values = [], []
    for i in range(7):
        keys.append(part(own, halo, i, K_F, TOK))
        values.append(part(own, halo, i, V_F, TOK).T)
    for a in range(4):
        query = own[a, Q_F : Q_F + TOK, :]
        ends = row_of(own[a, EXT:, :].astype(f32), 0).astype(jnp.int32)
        scores = []
        for b in range(a, a + REACH):
            s = nt(keys[b], query) * scale2
            if b < HALO:
                s = s - off
            if b == a + HALO:
                s = jnp.where(key_index <= ends, s, -FAR)
            scores.append(s)
        top = scores[0].max(0, keepdims=True)
        for s in scores[1:]:
            top = jnp.maximum(top, s.max(0, keepdims=True))
        total = jnp.zeros((1, TOK), f32)
        summed = jnp.zeros((HDIM, TOK), f32)
        for b, s in zip(range(a, a + REACH), scores):
            weights = jnp.exp2(s - top)
            total = total + weights.sum(0, keepdims=True)
            summed = summed + nn(values[b], weights.astype(bf16))
        out[a, :TOK, :] = (summed / total).T.astype(bf16)
        out[a, TOK:, :] = extra_rows(three_terms(top * LN2 + jnp.log(total)))


def backward_kernel(place, own, halo, g0, g1, g2, g3, forward_out, rest, grad_kv, ahead, grads):
    off = jnp.where(place[0] == 0, FAR, 0.0).astype(f32)
    scale2 = SCALE * LOG2E
    key_index = lax.broadcasted_iota(jnp.int32, (TOK, TOK), 0)
    rest[:, TOK:, :] = forward_out[...]
    for distance, ref in enumerate((g0, g1, g2, g3)):
        grads[lax.rem(place[1] + 4 - distance, 4)] = ref[...]

    extra = [own[i, EXT:, :].astype(f32) for i in range(4)]
    delta = [row_of(grads[i, TOK:GRAD_ROWS, :].astype(f32), 0, 3) for i in range(4)]
    totals = [row_of(extra[i], 2, 3) * LOG2E for i in range(4)]
    grad_query = [None] * 4
    for b in range(7):
        key = part(own, halo, b, K_B, TOK)
        value = part(own, halo, b, V_B, TOK)
        key_turned = key.T
        grad_key = grad_value = None
        for a in range(max(b - HALO, 0), min(b, HALO) + 1):
            query = own[a, Q_B : Q_B + TOK, :]
            grad = grads[a, :TOK, :]
            total = totals[a] + off if b < HALO else totals[a]
            weights = jnp.exp2(nt(key, query) * scale2 - total)
            if a + HALO == b:
                ends = row_of(extra[a], 1).astype(jnp.int32)
                weights = jnp.where(key_index <= ends, weights, 0.0)
            scores = (weights * (nt(value, grad) - delta[a])).astype(bf16)
            dk, dv = nn(scores, query), nn(weights.astype(bf16), grad)
            grad_key = dk if grad_key is None else grad_key + dk
            grad_value = dv if grad_value is None else grad_value + dv
            dq = nn(key_turned, scores)
            grad_query[a] = dq if grad_query[a] is None else grad_query[a] + dq
        if b <= HALO:
            grad_kv[b, :TOK, :] = grad_key * SCALE
            grad_kv[b, TOK:, :] = grad_value
        else:
            ahead[b - 4, :TOK, :] = (grad_key * SCALE).astype(bf16)
            ahead[b - 4, TOK:, :] = grad_value.astype(bf16)
    for a in range(4):
        rest[a, :TOK, :] = (grad_query[a] * SCALE).T.astype(bf16)


def finish_kernel(place, rest, grad_kv, behind, out0, out1, out2, out3, out):
    for b in range(4):
        total = grad_kv[b]
        if b < HALO:
            total = total + behind[b].astype(f32)
        out[b, : 2 * TOK, :] = total.astype(bf16)
        out[b, 2 * TOK :, :] = rest[b]
    for distance, ref in enumerate((out0, out1, out2, out3)):
        ref[...] = out[lax.rem(place[1] + distance, 4)]


def unpack_kernel(place, in0, in1, in2, in3, attended, log_total, grad_query, grad_keys, grad_values):
    for distance, ref in enumerate((in0, in1, in2, in3)):
        head = lax.rem(place[1] + 4 - distance, 4)
        lanes = pl.ds(pl.multiple_of(head * HDIM, HDIM), HDIM)
        grad_keys[:, lanes] = ref[:TOK, :].astype(f32)
        grad_values[:, lanes] = ref[TOK : 2 * TOK, :].astype(f32)
        grad_query[:, lanes] = ref[2 * TOK : 3 * TOK, :].astype(f32)
        attended[:, lanes] = ref[3 * TOK : 4 * TOK, :]
        extra = ref[4 * TOK :, :].astype(f32)
        log_total[pl.ds(head, 1), :] = row_of(extra, 0, 3)


def grad_kernel(place, c0, o0, c1, o1, c2, o2, c3, o3, weight, attn, g0, g1, g2, g3, out, grads):
    y_lo, y_hi, core = place[0], place[1], place[2]
    width = 4 * HDIM
    half = attn[:, pl.ds(pl.multiple_of(y_lo * TOK, TOK), TOK)].T
    half_far = c1[:, width:].T
    total = None
    for hi, side, near, far in ((0, 0, c0, c1), (0, 1, o0, o1), (1, 0, c2, c3), (1, 1, o2, o3)):
        y = y_hi + hi - 2 * y_hi * hi
        c = core + side - 2 * core * side
        group = 2 * y + c
        cot = near[:, :width]
        term = nt(cot, weight[:, pl.ds(pl.multiple_of(group * width, width), width)])
        total = term if total is None else total + term
        product = (nn(half, cot) + nn(half_far, far[:, :width])).astype(bf16)
        for j in range(4):
            out[group, j * TOK : (j + 1) * TOK, :] = product[:, j * HDIM : (j + 1) * HDIM]
    grad = total.astype(bf16)
    for head in range(4):
        lanes = slice(head * HDIM, (head + 1) * HDIM)
        product = grad[:, lanes].astype(f32) * attn[:, lanes].astype(f32)
        grads[head, :TOK, :] = grad[:, lanes]
        grads[head, TOK:GRAD_ROWS, :] = extra_rows(three_terms(product.T.sum(0, keepdims=True)))
    for distance, ref in enumerate((g0, g1, g2, g3)):
        ref[...] = grads[lax.rem(place[3] + distance, 4)]


def sum_kernel(parts, out):
    total = parts[0].astype(f32)
    for i in range(1, 4):
        total = total + parts[i].astype(f32)
    out[...] = total.astype(bf16)


def last_sum_kernel(parts, out):
    total = parts[0].astype(f32)
    for i in range(1, 8):
        total = total + parts[i].astype(f32)
    total = total.astype(bf16)
    for i in range(8):
        out[i] = total


def assemble_kernel(place, *refs):
    parts, (out, whole, sems) = refs[:8], refs[8:]
    copies = []
    strip = TOK // 4
    for far in range(2):
        y = place[0] + far - 2 * place[0] * far
        for piece in range(4):
            rows = pl.ds(pl.multiple_of(y * TOK + piece * strip, strip), strip)
            for distance in range(4):
                x = lax.rem(place[1] + 4 - distance, 4)
                ref = parts[far * 4 + distance]
                for j in range(4):
                    lanes = pl.ds(pl.multiple_of((x * 4 + j) * HDIM, HDIM), HDIM)
                    first = j * TOK + piece * strip
                    whole[rows, lanes] = ref[first : first + strip, :]
            copy = pltpu.make_async_copy(whole.at[rows], out.at[rows], sems.at[len(copies)])
            copy.start()
            copies.append(copy)
    for copy in copies:
        copy.wait()


def across(value, axes):
    return lax.all_to_all(value, axes, 0, 0, tiled=True)


def diagonal(value):
    return lax.ppermute(value, ("yl", "yh"), [(0, 3), (1, 2), (2, 1), (3, 0)])


def along_x(value, distance):
    return lax.ppermute(value, "x", [(i, (i + distance) % 4) for i in range(4)])


def next_row(value):
    return lax.ppermute(value, ("yl", "z"), [(i, (i + 1) % 16) for i in range(16)])


def other(value, axis):
    return lax.ppermute(value, axis, [(0, 1), (1, 0)])


def body(
    frames_fwd,
    query_fwd,
    keys_fwd,
    values_fwd,
    frames_bwd,
    query_bwd,
    keys_bwd,
    values_bwd,
    attn_bwd,
    logsumexp_bwd,
    cotangent,
    out_weight,
):
    y_lo = lax.axis_index("yl")
    place = jnp.stack([y_lo] + [lax.axis_index(axis) for axis in ("yh", "core", "x")]).astype(jnp.int32)
    place_x = jnp.stack([lax.axis_index(("yl", "z")), lax.axis_index("x")]).astype(jnp.int32)

    packed, to_pair = call(
        pack_kernel,
        [pltpu.HBM((4, BLOCK_ROWS, HDIM), bf16), pltpu.HBM((TOK, 6 * HDIM), bf16)],
        1,
        place,
        *map(in_hbm, (query_fwd, keys_fwd, values_fwd, keys_bwd, values_bwd, query_bwd)),
        *map(in_hbm, (logsumexp_bwd, attn_bwd, cotangent)),
        in_hbm(frames_fwd.reshape(1, TOK)),
        in_hbm(frames_bwd.reshape(1, TOK)),
        scratch=[
            pltpu.VMEM((4, BLOCK_ROWS, HDIM), bf16),
            pltpu.VMEM((TOK, 6 * HDIM), bf16),
            pltpu.SemaphoreType.DMA((5,)),
        ],
        raw_out=True,
    )
    cots = [cotangent, other(to_pair, "yl"), other(cotangent, "yh"), diagonal(cotangent)]
    own = across(packed, "x")
    halo = next_row(own[1:, HALO_FROM:Q_B, :])

    pairs = [(c, other(c, "core")) for c in cots]
    *grads, product = call(
        grad_kernel,
        [pltpu.HBM((GRAD_ROWS, HDIM), bf16)] * 4 + [pltpu.HBM((4, 4 * TOK, HDIM), bf16)],
        1,
        place,
        in_hbm(cotangent),
        *sum(pairs, ())[1:],
        in_hbm(out_weight),
        in_hbm(attn_bwd),
        scratch=[pltpu.VMEM((4, GRAD_ROWS, HDIM), bf16)],
    )
    products = across(product, "x")
    summed = call(sum_kernel, shape(4 * TOK, HDIM), 0, products)
    grads = [grads[0]] + [along_x(grads[d], d) for d in range(1, 4)]
    parts = across(summed.reshape(8, HDIM, HDIM), "z")
    forward_out = call(forward_kernel, shape(4, GRAD_ROWS, HDIM), 1, place_x, own, halo)
    parts, forward_out, grads = lax.optimization_barrier((parts, forward_out, grads))
    chunks = call(last_sum_kernel, pltpu.HBM((8, HDIM, HDIM), bf16), 0, parts)
    gathered = across(chunks, "z").reshape(4 * TOK, HDIM)
    rest, grad_kv, ahead = call(
        backward_kernel,
        [
            pltpu.HBM((4, TOK + GRAD_ROWS, HDIM), bf16),
            pltpu.HBM((4, 2 * TOK, HDIM), f32),
            pltpu.HBM((HALO, 2 * TOK, HDIM), bf16),
        ],
        1,
        place_x,
        own,
        halo,
        *map(in_hbm, grads),
        forward_out,
        scratch=[pltpu.VMEM((4, GRAD_ROWS, HDIM), bf16)],
    )
    behind = next_row(ahead)
    gathered, ahead = lax.optimization_barrier((gathered, ahead))
    row_parts = [gathered] + [along_x(gathered, d) for d in range(1, 4)]
    far_parts = [other(part, "yl") for part in row_parts]
    behind, row_parts, far_parts[0] = lax.optimization_barrier((behind, row_parts, far_parts[0]))
    outs = call(
        finish_kernel,
        [pltpu.HBM((BACK_ROWS, HDIM), bf16)] * 4,
        1,
        place_x,
        in_hbm(rest),
        in_hbm(grad_kv),
        behind,
        scratch=[pltpu.VMEM((4, BACK_ROWS, HDIM), bf16)],
    )
    back = [outs[0]] + [along_x(outs[d], d) for d in range(1, 4)]
    attended, log_total, grad_query, grad_keys, grad_values = call(
        unpack_kernel,
        [
            shape(TOK, 4 * HDIM),
            shape(4, TOK, dtype=f32),
            shape(TOK, 4 * HDIM, dtype=f32),
            shape(TOK, 4 * HDIM, dtype=f32),
            shape(TOK, 4 * HDIM, dtype=f32),
        ],
        1,
        place_x,
        *back,
    )
    place_xy = jnp.stack([y_lo, lax.axis_index("x")]).astype(jnp.int32)
    grad_weight = call(
        assemble_kernel,
        shape(2 * TOK, 16 * HDIM),
        1,
        place_xy,
        *row_parts,
        *far_parts,
        scratch=[pltpu.VMEM((2 * TOK, 16 * HDIM), bf16), pltpu.SemaphoreType.DMA((8,))],
        raw_out=True,
    )
    return (attended, log_total, grad_query, grad_keys, grad_values, grad_weight)


def solution(mesh):
    fine = Mesh(mesh.devices.reshape(2, 8, 4, 2, 2), ("yl", "z", "x", "yh", "core"))
    ctx, dp = ("yl", "z", "x"), ("yh", "core")
    in_specs = (
        P(ctx),
        P(ctx, dp),
        P(ctx, dp),
        P(ctx, dp),
        P(ctx),
        P(ctx, dp),
        P(ctx, dp),
        P(ctx, dp),
        P(ctx, dp),
        P(dp, ctx),
        P(ctx, dp),
        P(dp, None),
    )
    out_specs = (
        P(ctx, dp),
        P(dp, ctx),
        P(ctx, dp),
        P(ctx, dp),
        P(ctx, dp),
        P(dp, None),
    )
    return jax.shard_map(body, mesh=fine, in_specs=in_specs, out_specs=out_specs, check_vma=False)
```

```python
import math

import jax
import jax.numpy as jnp
from jax import lax
from jax.experimental import pallas as pl
from jax.experimental.pallas import tpu as pltpu
from jax.sharding import Mesh
from jax.sharding import PartitionSpec as P

HDIM = 128
TOK = 256
REACH = 4
HALO = REACH - 1
SCALE = 1.0 / math.sqrt(HDIM)
LOG2E = math.log2(math.e)
LN2 = math.log(2.0)
FAR = 1e30
EXTRA = 16
VMEM_BYTES = 48 * 1024 * 1024

f32 = jnp.float32
bf16 = jnp.bfloat16

Q_F, K_F, V_F, K_B, V_B, Q_B, EXT = (TOK * i for i in range(7))
BLOCK_ROWS = EXT + EXTRA
HALO_FROM = K_F
GRAD_ROWS = TOK + EXTRA
BACK_ROWS = 4 * TOK + EXTRA


def nt(a, b):
    return lax.dot_general(a, b, (((1,), (1,)), ((), ())), preferred_element_type=f32)


def nn(a, b):
    return lax.dot_general(a, b, (((1,), (0,)), ((), ())), preferred_element_type=f32)


def three_terms(value):
    high = value.astype(bf16).astype(f32)
    rest = value - high
    middle = rest.astype(bf16).astype(f32)
    return [high, middle, rest - middle]


def extra_rows(rows):
    halves = []
    for row in rows:
        halves += [row[:, :HDIM], row[:, HDIM:]]
    halves += [jnp.zeros((EXTRA - len(halves), HDIM), f32)]
    return jnp.concatenate(halves, axis=0).astype(bf16)


def row_of(extra, first, count=1):
    total = None
    for i in range(first, first + count):
        row = jnp.concatenate([extra[2 * i : 2 * i + 1], extra[2 * i + 1 : 2 * i + 2]], axis=1)
        total = row if total is None else total + row
    return total


def in_hbm(value):
    return pltpu.with_memory_space_constraint(value, pltpu.HBM)


def call(kernel, out_shape, n_smem, *args, scratch=(), raw_in=(), raw_out=False):
    spaces = [pltpu.SMEM] * n_smem + [pltpu.VMEM] * (len(args) - n_smem)
    for i in raw_in:
        spaces[i] = pltpu.HBM
    single = not isinstance(out_shape, (tuple, list))
    out_space = pl.BlockSpec(memory_space=pltpu.HBM if raw_out else pltpu.VMEM)
    return pl.pallas_call(
        kernel,
        out_shape=out_shape,
        in_specs=[pl.BlockSpec(memory_space=space) for space in spaces],
        scratch_shapes=scratch,
        out_specs=out_space if single else [out_space] * len(out_shape),
        compiler_params=pltpu.CompilerParams(vmem_limit_bytes=VMEM_BYTES),
    )(*args)


def shape(*dims, dtype=bf16):
    return jax.ShapeDtypeStruct(dims, dtype)


def block_ends(frames):
    across_lanes = jnp.broadcast_to(frames, (TOK, TOK))
    seen = jnp.where(across_lanes.T <= across_lanes, 1.0, 0.0)
    return seen.sum(0, keepdims=True) - 1.0


def pack_kernel(
    place, qf, kf, vf, kb, vb, qb, lse, attn, cot, frames_fwd, frames_bwd, out, to_pair, packed, paired, sems
):
    far_half = pl.multiple_of((1 - place[0]) * TOK, TOK)
    paired[:, : 4 * HDIM] = cot[...]
    paired[:, 4 * HDIM :] = attn[:, pl.ds(far_half, TOK)]
    copies = [pltpu.make_async_copy(paired, to_pair, sems.at[4])]
    copies[0].start()
    ends = [block_ends(frames_fwd[...].astype(f32)), block_ends(frames_bwd[...].astype(f32))]
    for head in range(4):
        lanes = slice(head * HDIM, (head + 1) * HDIM)
        for i, ref in enumerate((qf, kf, vf, kb, vb, qb)):
            packed[head, i * TOK : (i + 1) * TOK, :] = ref[:, lanes]
        rows = ends + three_terms(lse[head : head + 1, :])
        packed[head, EXT:, :] = extra_rows(rows)
        copy = pltpu.make_async_copy(packed.at[head], out.at[head], sems.at[head])
        copy.start()
        copies.append(copy)
    for copy in copies:
        copy.wait()


def part(own, halo, index, first, rows):
    if index < HALO:
        return halo[index, first - HALO_FROM : first - HALO_FROM + rows, :]
    return own[index - HALO, first : first + rows, :]


def forward_kernel(place, own, halo, out):
    off = jnp.where(place[0] == 0, FAR, 0.0).astype(f32)
    scale2 = SCALE * LOG2E
    key_index = lax.broadcasted_iota(jnp.int32, (TOK, TOK), 0)
    keys, values = [], []
    for i in range(7):
        keys.append(part(own, halo, i, K_F, TOK))
        values.append(part(own, halo, i, V_F, TOK).T)
    for a in range(4):
        query = own[a, Q_F : Q_F + TOK, :]
        ends = row_of(own[a, EXT:, :].astype(f32), 0).astype(jnp.int32)
        scores = []
        for b in range(a, a + REACH):
            s = nt(keys[b], query) * scale2
            if b < HALO:
                s = s - off
            if b == a + HALO:
                s = jnp.where(key_index <= ends, s, -FAR)
            scores.append(s)
        top = scores[0].max(0, keepdims=True)
        for s in scores[1:]:
            top = jnp.maximum(top, s.max(0, keepdims=True))
        total = jnp.zeros((1, TOK), f32)
        summed = jnp.zeros((HDIM, TOK), f32)
        for b, s in zip(range(a, a + REACH), scores):
            weights = jnp.exp2(s - top)
            total = total + weights.sum(0, keepdims=True)
            summed = summed + nn(values[b], weights.astype(bf16))
        out[a, :TOK, :] = (summed / total).T.astype(bf16)
        out[a, TOK:, :] = extra_rows(three_terms(top * LN2 + jnp.log(total)))


def backward_kernel(place, own, halo, g0, g1, g2, g3, forward_out, rest, grad_kv, ahead, grads):
    off = jnp.where(place[0] == 0, FAR, 0.0).astype(f32)
    scale2 = SCALE * LOG2E
    key_index = lax.broadcasted_iota(jnp.int32, (TOK, TOK), 0)
    rest[:, TOK:, :] = forward_out[...]
    for distance, ref in enumerate((g0, g1, g2, g3)):
        grads[lax.rem(place[1] + 4 - distance, 4)] = ref[...]

    extra = [own[i, EXT:, :].astype(f32) for i in range(4)]
    delta = [row_of(grads[i, TOK:GRAD_ROWS, :].astype(f32), 0, 3) for i in range(4)]
    totals = [row_of(extra[i], 2, 3) * LOG2E for i in range(4)]
    grad_query = [None] * 4
    for b in range(7):
        key = part(own, halo, b, K_B, TOK)
        value = part(own, halo, b, V_B, TOK)
        key_turned = key.T
        grad_key = grad_value = None
        for a in range(max(b - HALO, 0), min(b, HALO) + 1):
            query = own[a, Q_B : Q_B + TOK, :]
            grad = grads[a, :TOK, :]
            total = totals[a] + off if b < HALO else totals[a]
            weights = jnp.exp2(nt(key, query) * scale2 - total)
            if a + HALO == b:
                ends = row_of(extra[a], 1).astype(jnp.int32)
                weights = jnp.where(key_index <= ends, weights, 0.0)
            scores = (weights * (nt(value, grad) - delta[a])).astype(bf16)
            dk, dv = nn(scores, query), nn(weights.astype(bf16), grad)
            grad_key = dk if grad_key is None else grad_key + dk
            grad_value = dv if grad_value is None else grad_value + dv
            dq = nn(key_turned, scores)
            grad_query[a] = dq if grad_query[a] is None else grad_query[a] + dq
        if b <= HALO:
            grad_kv[b, :TOK, :] = grad_key * SCALE
            grad_kv[b, TOK:, :] = grad_value
        else:
            ahead[b - 4, :TOK, :] = (grad_key * SCALE).astype(bf16)
            ahead[b - 4, TOK:, :] = grad_value.astype(bf16)
    for a in range(4):
        rest[a, :TOK, :] = (grad_query[a] * SCALE).T.astype(bf16)


def finish_kernel(place, rest, grad_kv, behind, out0, out1, out2, out3, out):
    for b in range(4):
        total = grad_kv[b]
        if b < HALO:
            total = total + behind[b].astype(f32)
        out[b, : 2 * TOK, :] = total.astype(bf16)
        out[b, 2 * TOK :, :] = rest[b]
    for distance, ref in enumerate((out0, out1, out2, out3)):
        ref[...] = out[lax.rem(place[1] + distance, 4)]


def grad_kernel(place, c0, o0, c1, o1, c2, o2, c3, o3, weight, attn, g0, g1, g2, g3, out, grads):
    y_lo, y_hi, core = place[0], place[1], place[2]
    width = 4 * HDIM
    half = attn[:, pl.ds(pl.multiple_of(y_lo * TOK, TOK), TOK)].T
    half_far = c1[:, width:].T
    total = None
    for hi, side, near, far in ((0, 0, c0, c1), (0, 1, o0, o1), (1, 0, c2, c3), (1, 1, o2, o3)):
        y = y_hi + hi - 2 * y_hi * hi
        c = core + side - 2 * core * side
        group = 2 * y + c
        cot = near[:, :width]
        term = nt(cot, weight[:, pl.ds(pl.multiple_of(group * width, width), width)])
        total = term if total is None else total + term
        product = (nn(half, cot) + nn(half_far, far[:, :width])).astype(bf16)
        for j in range(4):
            out[group, j * TOK : (j + 1) * TOK, :] = product[:, j * HDIM : (j + 1) * HDIM]
    grad = total.astype(bf16)
    for head in range(4):
        lanes = slice(head * HDIM, (head + 1) * HDIM)
        product = grad[:, lanes].astype(f32) * attn[:, lanes].astype(f32)
        grads[head, :TOK, :] = grad[:, lanes]
        grads[head, TOK:GRAD_ROWS, :] = extra_rows(three_terms(product.T.sum(0, keepdims=True)))
    for distance, ref in enumerate((g0, g1, g2, g3)):
        ref[...] = grads[lax.rem(place[3] + distance, 4)]


def sum_kernel(parts, out):
    total = parts[0].astype(f32)
    for i in range(1, 4):
        total = total + parts[i].astype(f32)
    out[...] = total.astype(bf16)


def last_sum_kernel(parts, out):
    total = parts[0].astype(f32)
    for i in range(1, 8):
        total = total + parts[i].astype(f32)
    total = total.astype(bf16)
    for i in range(8):
        out[i] = total


def last_kernel(place, *refs):
    back, near_parts, far_parts = refs[:4], refs[4:8], refs[8:13]
    attended, log_total, grad_query, grad_keys, grad_values, out = refs[13:19]
    held, held_attended, held_total, whole, sems = refs[19:]

    def part_rows(far, distance, rows):
        if not far:
            return near_parts[distance][rows, :]
        if distance:
            return far_parts[distance + 1][rows, :]
        return jnp.where(place[3] == 1, far_parts[0][rows, :], far_parts[1][rows, :])

    copies = []

    def send(source, target):
        copies.append(pltpu.make_async_copy(source, target, sems.at[len(copies)]))
        copies[-1].start()

    for i, target in enumerate((grad_keys, grad_values, grad_query)):
        for distance, ref in enumerate(back):
            head = lax.rem(place[1] + 4 - distance, 4)
            lanes = pl.ds(pl.multiple_of(head * HDIM, HDIM), HDIM)
            held[i, :, lanes] = ref[i * TOK : (i + 1) * TOK, :].astype(f32)
        send(held.at[i], target)
    for distance, ref in enumerate(back):
        head = lax.rem(place[1] + 4 - distance, 4)
        lanes = pl.ds(pl.multiple_of(head * HDIM, HDIM), HDIM)
        held_attended[:, lanes] = ref[3 * TOK : 4 * TOK, :]
        held_total[pl.ds(head, 1), :] = row_of(ref[4 * TOK :, :].astype(f32), 0, 3)
    send(held_attended, attended)
    send(held_total, log_total)
    strip = TOK // 4
    for far in range(2):
        y = place[2] + far - 2 * place[2] * far
        for piece in range(4):
            rows = pl.ds(pl.multiple_of(y * TOK + piece * strip, strip), strip)
            for distance in range(4):
                x = lax.rem(place[1] + 4 - distance, 4)
                for j in range(4):
                    lanes = pl.ds(pl.multiple_of((x * 4 + j) * HDIM, HDIM), HDIM)
                    first = j * TOK + piece * strip
                    whole[rows, lanes] = part_rows(far, distance, slice(first, first + strip))
            send(whole.at[rows], out.at[rows])
    for copy in copies:
        copy.wait()


def across(value, axes):
    return lax.all_to_all(value, axes, 0, 0, tiled=True)


def diagonal(value):
    return lax.ppermute(value, ("yl", "yh"), [(0, 3), (1, 2), (2, 1), (3, 0)])


def along_x(value, distance):
    return lax.ppermute(value, "x", [(i, (i + distance) % 4) for i in range(4)])


def across_y(value, parities=(0, 1)):
    pairs = [(y * 8 + z, (1 - y) * 8 + z) for y in range(2) for z in range(8) if z % 2 in parities]
    return lax.ppermute(value, ("yl", "z"), pairs)


def beside(value, parity):
    return lax.ppermute(value, "z", [(z, z ^ 1) for z in range(8) if z % 2 == parity])


def next_row(value):
    return lax.ppermute(value, ("yl", "z"), [(i, (i + 1) % 16) for i in range(16)])


def other(value, axis):
    return lax.ppermute(value, axis, [(0, 1), (1, 0)])


def body(
    frames_fwd,
    query_fwd,
    keys_fwd,
    values_fwd,
    frames_bwd,
    query_bwd,
    keys_bwd,
    values_bwd,
    attn_bwd,
    logsumexp_bwd,
    cotangent,
    out_weight,
):
    y_lo = lax.axis_index("yl")
    place = jnp.stack([y_lo] + [lax.axis_index(axis) for axis in ("yh", "core", "x")]).astype(jnp.int32)
    place_x = jnp.stack(
        [lax.axis_index(("yl", "z")), lax.axis_index("x"), y_lo, lax.rem(lax.axis_index("z"), 2)]
    ).astype(jnp.int32)

    packed, to_pair = call(
        pack_kernel,
        [pltpu.HBM((4, BLOCK_ROWS, HDIM), bf16), pltpu.HBM((TOK, 6 * HDIM), bf16)],
        1,
        place,
        *map(in_hbm, (query_fwd, keys_fwd, values_fwd, keys_bwd, values_bwd, query_bwd)),
        *map(in_hbm, (logsumexp_bwd, attn_bwd, cotangent)),
        in_hbm(frames_fwd.reshape(1, TOK)),
        in_hbm(frames_bwd.reshape(1, TOK)),
        scratch=[
            pltpu.VMEM((4, BLOCK_ROWS, HDIM), bf16),
            pltpu.VMEM((TOK, 6 * HDIM), bf16),
            pltpu.SemaphoreType.DMA((5,)),
        ],
        raw_out=True,
    )
    cots = [cotangent, other(to_pair, "yl"), other(cotangent, "yh"), diagonal(cotangent)]
    own = across(packed, "x")
    halo = next_row(own[1:, HALO_FROM:Q_B, :])

    pairs = [(c, other(c, "core")) for c in cots]
    *grads, product = call(
        grad_kernel,
        [pltpu.HBM((GRAD_ROWS, HDIM), bf16)] * 4 + [pltpu.HBM((4, 4 * TOK, HDIM), bf16)],
        1,
        place,
        in_hbm(cotangent),
        *sum(pairs, ())[1:],
        in_hbm(out_weight),
        in_hbm(attn_bwd),
        scratch=[pltpu.VMEM((4, GRAD_ROWS, HDIM), bf16)],
    )
    products = across(product, "x")
    summed = call(sum_kernel, pltpu.HBM((4 * TOK, HDIM), bf16), 0, products)
    grads = [grads[0]] + [along_x(grads[d], d) for d in range(1, 4)]
    parts = across(summed.reshape(8, HDIM, HDIM), "z")
    forward_out = call(forward_kernel, shape(4, GRAD_ROWS, HDIM), 1, place_x, own, halo)
    parts, forward_out, grads = lax.optimization_barrier((parts, forward_out, grads))
    chunks = call(last_sum_kernel, pltpu.HBM((8, HDIM, HDIM), bf16), 0, parts)
    gathered = across(chunks, "z").reshape(4 * TOK, HDIM)
    rest, grad_kv, ahead = call(
        backward_kernel,
        [
            pltpu.HBM((4, TOK + GRAD_ROWS, HDIM), bf16),
            pltpu.HBM((4, 2 * TOK, HDIM), f32),
            pltpu.HBM((HALO, 2 * TOK, HDIM), bf16),
        ],
        1,
        place_x,
        own,
        halo,
        *map(in_hbm, grads),
        forward_out,
        scratch=[pltpu.VMEM((4, GRAD_ROWS, HDIM), bf16)],
    )
    behind = next_row(ahead)
    gathered, ahead = lax.optimization_barrier((gathered, ahead))
    row_parts = [gathered] + [along_x(gathered, d) for d in range(1, 4)]
    crossed = across_y(row_parts[0], (1,))
    far_parts = [crossed, beside(crossed, 1)] + [across_y(part) for part in row_parts[1:]]
    behind, row_parts[3] = lax.optimization_barrier((behind, row_parts[3]))
    outs = call(
        finish_kernel,
        [pltpu.HBM((BACK_ROWS, HDIM), bf16)] * 4,
        1,
        place_x,
        in_hbm(rest),
        in_hbm(grad_kv),
        behind,
        scratch=[pltpu.VMEM((4, BACK_ROWS, HDIM), bf16)],
    )
    back = [outs[0]] + [along_x(outs[d], d) for d in range(1, 4)]
    block = (TOK, 4 * HDIM)
    return tuple(
        call(
            last_kernel,
            [
                shape(*block),
                shape(4, TOK, dtype=f32),
                shape(*block, dtype=f32),
                shape(*block, dtype=f32),
                shape(*block, dtype=f32),
                shape(2 * TOK, 16 * HDIM),
            ],
            1,
            place_x,
            in_hbm(back[0]),
            *back[1:],
            *row_parts,
            *far_parts,
            scratch=[
                pltpu.VMEM((3, *block), f32),
                pltpu.VMEM(block, bf16),
                pltpu.VMEM((4, TOK), f32),
                pltpu.VMEM((2 * TOK, 16 * HDIM), bf16),
                pltpu.SemaphoreType.DMA((13,)),
            ],
            raw_out=True,
        )
    )


def solution(mesh):
    fine = Mesh(mesh.devices.reshape(2, 8, 4, 2, 2), ("yl", "z", "x", "yh", "core"))
    ctx, dp = ("yl", "z", "x"), ("yh", "core")
    in_specs = (
        P(ctx),
        P(ctx, dp),
        P(ctx, dp),
        P(ctx, dp),
        P(ctx),
        P(ctx, dp),
        P(ctx, dp),
        P(ctx, dp),
        P(ctx, dp),
        P(dp, ctx),
        P(ctx, dp),
        P(dp, None),
    )
    out_specs = (
        P(ctx, dp),
        P(dp, ctx),
        P(ctx, dp),
        P(ctx, dp),
        P(ctx, dp),
        P(dp, None),
    )
    return jax.shard_map(body, mesh=fine, in_specs=in_specs, out_specs=out_specs, check_vma=False)
```

```python
import math

import jax
import jax.numpy as jnp
from jax import lax
from jax.experimental import pallas as pl
from jax.experimental.pallas import tpu as pltpu
from jax.sharding import Mesh
from jax.sharding import PartitionSpec as P

HDIM = 128
TOK = 256
REACH = 4
HALO = REACH - 1
SCALE = 1.0 / math.sqrt(HDIM)
LOG2E = math.log2(math.e)
LN2 = math.log(2.0)
FAR = 1e30
EXTRA = 16
VMEM_BYTES = 48 * 1024 * 1024

f32 = jnp.float32
bf16 = jnp.bfloat16

Q_F, K_F, V_F, K_B, V_B, Q_B, EXT = (TOK * i for i in range(7))
BLOCK_ROWS = EXT + EXTRA
HALO_FROM = K_F
GRAD_ROWS = TOK + EXTRA
BACK_ROWS = 4 * TOK + EXTRA


def nt(a, b):
    return lax.dot_general(a, b, (((1,), (1,)), ((), ())), preferred_element_type=f32)


def nn(a, b):
    return lax.dot_general(a, b, (((1,), (0,)), ((), ())), preferred_element_type=f32)


def three_terms(value):
    high = value.astype(bf16).astype(f32)
    rest = value - high
    middle = rest.astype(bf16).astype(f32)
    return [high, middle, rest - middle]


def extra_rows(rows):
    halves = []
    for row in rows:
        halves += [row[:, :HDIM], row[:, HDIM:]]
    halves += [jnp.zeros((EXTRA - len(halves), HDIM), f32)]
    return jnp.concatenate(halves, axis=0).astype(bf16)


def row_of(extra, first, count=1):
    total = None
    for i in range(first, first + count):
        row = jnp.concatenate([extra[2 * i : 2 * i + 1], extra[2 * i + 1 : 2 * i + 2]], axis=1)
        total = row if total is None else total + row
    return total


def in_hbm(value):
    return pltpu.with_memory_space_constraint(value, pltpu.HBM)


def call(kernel, out_shape, n_smem, *args, scratch=(), raw_in=(), raw_out=False):
    spaces = [pltpu.SMEM] * n_smem + [pltpu.VMEM] * (len(args) - n_smem)
    for i in raw_in:
        spaces[i] = pltpu.HBM
    single = not isinstance(out_shape, (tuple, list))
    out_space = pl.BlockSpec(memory_space=pltpu.HBM if raw_out else pltpu.VMEM)
    return pl.pallas_call(
        kernel,
        out_shape=out_shape,
        in_specs=[pl.BlockSpec(memory_space=space) for space in spaces],
        scratch_shapes=scratch,
        out_specs=out_space if single else [out_space] * len(out_shape),
        compiler_params=pltpu.CompilerParams(vmem_limit_bytes=VMEM_BYTES),
    )(*args)


def shape(*dims, dtype=bf16):
    return jax.ShapeDtypeStruct(dims, dtype)


def block_ends(frames):
    across_lanes = jnp.broadcast_to(frames, (TOK, TOK))
    seen = jnp.where(across_lanes.T <= across_lanes, 1.0, 0.0)
    return seen.sum(0, keepdims=True) - 1.0


def pack_kernel(
    place, qf, kf, vf, kb, vb, qb, lse, attn, cot, frames_fwd, frames_bwd, out, to_pair, packed, paired, sems
):
    far_half = pl.multiple_of((1 - place[0]) * TOK, TOK)
    paired[:, : 4 * HDIM] = cot[...]
    paired[:, 4 * HDIM :] = attn[:, pl.ds(far_half, TOK)]
    copies = [pltpu.make_async_copy(paired, to_pair, sems.at[4])]
    copies[0].start()
    ends = [block_ends(frames_fwd[...].astype(f32)), block_ends(frames_bwd[...].astype(f32))]
    for head in range(4):
        lanes = slice(head * HDIM, (head + 1) * HDIM)
        for i, ref in enumerate((qf, kf, vf, kb, vb, qb)):
            packed[head, i * TOK : (i + 1) * TOK, :] = ref[:, lanes]
        rows = ends + three_terms(lse[head : head + 1, :])
        packed[head, EXT:, :] = extra_rows(rows)
        copy = pltpu.make_async_copy(packed.at[head], out.at[head], sems.at[head])
        copy.start()
        copies.append(copy)
    for copy in copies:
        copy.wait()


def part(own, halo, index, first, rows):
    if index < HALO:
        return halo[index, first - HALO_FROM : first - HALO_FROM + rows, :]
    return own[index - HALO, first : first + rows, :]


def forward_kernel(place, own, halo, out):
    off = jnp.where(place[0] == 0, FAR, 0.0).astype(f32)
    scale2 = SCALE * LOG2E
    key_index = lax.broadcasted_iota(jnp.int32, (TOK, TOK), 0)
    keys, values = [], []
    for i in range(7):
        keys.append(part(own, halo, i, K_F, TOK))
        values.append(part(own, halo, i, V_F, TOK).T)
    for a in range(4):
        query = own[a, Q_F : Q_F + TOK, :]
        ends = row_of(own[a, EXT:, :].astype(f32), 0).astype(jnp.int32)
        scores = []
        for b in range(a, a + REACH):
            s = nt(keys[b], query) * scale2
            if b < HALO:
                s = s - off
            if b == a + HALO:
                s = jnp.where(key_index <= ends, s, -FAR)
            scores.append(s)
        top = scores[0].max(0, keepdims=True)
        for s in scores[1:]:
            top = jnp.maximum(top, s.max(0, keepdims=True))
        total = jnp.zeros((1, TOK), f32)
        summed = jnp.zeros((HDIM, TOK), f32)
        for b, s in zip(range(a, a + REACH), scores):
            weights = jnp.exp2(s - top)
            total = total + weights.sum(0, keepdims=True)
            summed = summed + nn(values[b], weights.astype(bf16))
        out[a, :TOK, :] = (summed / total).T.astype(bf16)
        out[a, TOK:, :] = extra_rows(three_terms(top * LN2 + jnp.log(total)))


def backward_kernel(place, own, halo, g0, g1, g2, g3, forward_out, rest, grad_kv, ahead, grads):
    off = jnp.where(place[0] == 0, FAR, 0.0).astype(f32)
    scale2 = SCALE * LOG2E
    key_index = lax.broadcasted_iota(jnp.int32, (TOK, TOK), 0)
    rest[:, TOK:, :] = forward_out[...]
    for distance, ref in enumerate((g0, g1, g2, g3)):
        grads[lax.rem(place[1] + 4 - distance, 4)] = ref[...]

    extra = [own[i, EXT:, :].astype(f32) for i in range(4)]
    delta = [row_of(grads[i, TOK:GRAD_ROWS, :].astype(f32), 0, 3) for i in range(4)]
    totals = [row_of(extra[i], 2, 3) * LOG2E for i in range(4)]
    grad_query = [None] * 4
    for b in range(7):
        key = part(own, halo, b, K_B, TOK)
        value = part(own, halo, b, V_B, TOK)
        key_turned = key.T
        grad_key = grad_value = None
        for a in range(max(b - HALO, 0), min(b, HALO) + 1):
            query = own[a, Q_B : Q_B + TOK, :]
            grad = grads[a, :TOK, :]
            total = totals[a] + off if b < HALO else totals[a]
            weights = jnp.exp2(nt(key, query) * scale2 - total)
            if a + HALO == b:
                ends = row_of(extra[a], 1).astype(jnp.int32)
                weights = jnp.where(key_index <= ends, weights, 0.0)
            scores = (weights * (nt(value, grad) - delta[a])).astype(bf16)
            dk, dv = nn(scores, query), nn(weights.astype(bf16), grad)
            grad_key = dk if grad_key is None else grad_key + dk
            grad_value = dv if grad_value is None else grad_value + dv
            dq = nn(key_turned, scores)
            grad_query[a] = dq if grad_query[a] is None else grad_query[a] + dq
        if b <= HALO:
            grad_kv[b, :TOK, :] = grad_key * SCALE
            grad_kv[b, TOK:, :] = grad_value
        else:
            ahead[b - 4, :TOK, :] = (grad_key * SCALE).astype(bf16)
            ahead[b - 4, TOK:, :] = grad_value.astype(bf16)
    for a in range(4):
        rest[a, :TOK, :] = (grad_query[a] * SCALE).T.astype(bf16)


def finish_kernel(place, rest, grad_kv, behind, out0, out1, out2, out3, out):
    for b in range(4):
        total = grad_kv[b]
        if b < HALO:
            total = total + behind[b].astype(f32)
        out[b, : 2 * TOK, :] = total.astype(bf16)
        out[b, 2 * TOK :, :] = rest[b]
    for distance, ref in enumerate((out0, out1, out2, out3)):
        ref[...] = out[lax.rem(place[1] + distance, 4)]


def grad_kernel(place, c0, o0, c1, o1, c2, o2, c3, o3, weight, attn, g0, g1, g2, g3, out, grads):
    y_lo, y_hi, core = place[0], place[1], place[2]
    width = 4 * HDIM
    half = attn[:, pl.ds(pl.multiple_of(y_lo * TOK, TOK), TOK)].T
    half_far = c1[:, width:].T
    total = None
    for hi, side, near, far in ((0, 0, c0, c1), (0, 1, o0, o1), (1, 0, c2, c3), (1, 1, o2, o3)):
        y = y_hi + hi - 2 * y_hi * hi
        c = core + side - 2 * core * side
        group = 2 * y + c
        cot = near[:, :width]
        term = nt(cot, weight[:, pl.ds(pl.multiple_of(group * width, width), width)])
        total = term if total is None else total + term
        product = (nn(half, cot) + nn(half_far, far[:, :width])).astype(bf16)
        for j in range(4):
            out[group, j * TOK : (j + 1) * TOK, :] = product[:, j * HDIM : (j + 1) * HDIM]
    grad = total.astype(bf16)
    for head in range(4):
        lanes = slice(head * HDIM, (head + 1) * HDIM)
        product = grad[:, lanes].astype(f32) * attn[:, lanes].astype(f32)
        grads[head, :TOK, :] = grad[:, lanes]
        grads[head, TOK:GRAD_ROWS, :] = extra_rows(three_terms(product.T.sum(0, keepdims=True)))
    for distance, ref in enumerate((g0, g1, g2, g3)):
        ref[...] = grads[lax.rem(place[3] + distance, 4)]


def sum_kernel(parts, out):
    total = parts[0].astype(f32)
    for i in range(1, 4):
        total = total + parts[i].astype(f32)
    out[...] = total.astype(bf16)


def last_sum_kernel(parts, out):
    total = parts[0].astype(f32)
    for i in range(1, 8):
        total = total + parts[i].astype(f32)
    total = total.astype(bf16)
    for i in range(8):
        out[i] = total


def last_kernel(place, *refs):
    back, near_parts, far_parts = refs[:4], refs[4:8], refs[8:13]
    attended, log_total, grad_query, grad_keys, grad_values, out = refs[13:19]
    held, held_attended, held_total, whole, own_back, sems = refs[19:]
    load = pltpu.make_async_copy(back[0], own_back, sems.at[13])
    load.start()

    def part_rows(far, distance, rows):
        if not far:
            return near_parts[distance][rows, :]
        if distance:
            return far_parts[distance + 1][rows, :]
        return jnp.where(place[3] == 1, far_parts[0][rows, :], far_parts[1][rows, :])

    copies = []

    def send(source, target):
        copies.append(pltpu.make_async_copy(source, target, sems.at[len(copies)]))
        copies[-1].start()

    strip = TOK // 4
    for far in range(2):
        y = place[2] + far - 2 * place[2] * far
        for piece in range(4):
            rows = pl.ds(pl.multiple_of(y * TOK + piece * strip, strip), strip)
            for distance in range(4):
                x = lax.rem(place[1] + 4 - distance, 4)
                for j in range(4):
                    lanes = pl.ds(pl.multiple_of((x * 4 + j) * HDIM, HDIM), HDIM)
                    first = j * TOK + piece * strip
                    whole[rows, lanes] = part_rows(far, distance, slice(first, first + strip))
            send(whole.at[rows], out.at[rows])
    load.wait()
    back = (own_back, *back[1:])
    for i, target in enumerate((grad_keys, grad_values, grad_query)):
        for distance, ref in enumerate(back):
            head = lax.rem(place[1] + 4 - distance, 4)
            lanes = pl.ds(pl.multiple_of(head * HDIM, HDIM), HDIM)
            held[i, :, lanes] = ref[i * TOK : (i + 1) * TOK, :].astype(f32)
        send(held.at[i], target)
    for distance, ref in enumerate(back):
        head = lax.rem(place[1] + 4 - distance, 4)
        lanes = pl.ds(pl.multiple_of(head * HDIM, HDIM), HDIM)
        held_attended[:, lanes] = ref[3 * TOK : 4 * TOK, :]
        held_total[pl.ds(head, 1), :] = row_of(ref[4 * TOK :, :].astype(f32), 0, 3)
    send(held_attended, attended)
    send(held_total, log_total)
    for copy in copies:
        copy.wait()


def across(value, axes):
    return lax.all_to_all(value, axes, 0, 0, tiled=True)


def diagonal(value):
    return lax.ppermute(value, ("yl", "yh"), [(0, 3), (1, 2), (2, 1), (3, 0)])


def along_x(value, distance):
    return lax.ppermute(value, "x", [(i, (i + distance) % 4) for i in range(4)])


def across_y(value, parities=(0, 1)):
    pairs = [(y * 8 + z, (1 - y) * 8 + z) for y in range(2) for z in range(8) if z % 2 in parities]
    return lax.ppermute(value, ("yl", "z"), pairs)


def beside(value, parity):
    return lax.ppermute(value, "z", [(z, z ^ 1) for z in range(8) if z % 2 == parity])


def next_row(value):
    return lax.ppermute(value, ("yl", "z"), [(i, (i + 1) % 16) for i in range(16)])


def other(value, axis):
    return lax.ppermute(value, axis, [(0, 1), (1, 0)])


def body(
    frames_fwd,
    query_fwd,
    keys_fwd,
    values_fwd,
    frames_bwd,
    query_bwd,
    keys_bwd,
    values_bwd,
    attn_bwd,
    logsumexp_bwd,
    cotangent,
    out_weight,
):
    y_lo = lax.axis_index("yl")
    place = jnp.stack([y_lo] + [lax.axis_index(axis) for axis in ("yh", "core", "x")]).astype(jnp.int32)
    place_x = jnp.stack(
        [lax.axis_index(("yl", "z")), lax.axis_index("x"), y_lo, lax.rem(lax.axis_index("z"), 2)]
    ).astype(jnp.int32)

    packed, to_pair = call(
        pack_kernel,
        [pltpu.HBM((4, BLOCK_ROWS, HDIM), bf16), pltpu.HBM((TOK, 6 * HDIM), bf16)],
        1,
        place,
        *map(in_hbm, (query_fwd, keys_fwd, values_fwd, keys_bwd, values_bwd, query_bwd)),
        *map(in_hbm, (logsumexp_bwd, attn_bwd, cotangent)),
        in_hbm(frames_fwd.reshape(1, TOK)),
        in_hbm(frames_bwd.reshape(1, TOK)),
        scratch=[
            pltpu.VMEM((4, BLOCK_ROWS, HDIM), bf16),
            pltpu.VMEM((TOK, 6 * HDIM), bf16),
            pltpu.SemaphoreType.DMA((5,)),
        ],
        raw_out=True,
    )
    cots = [cotangent, other(to_pair, "yl"), other(cotangent, "yh"), diagonal(cotangent)]
    own = across(packed, "x")
    halo = next_row(own[1:, HALO_FROM:Q_B, :])

    pairs = [(c, other(c, "core")) for c in cots]
    *grads, product = call(
        grad_kernel,
        [pltpu.HBM((GRAD_ROWS, HDIM), bf16)] * 4 + [pltpu.HBM((4, 4 * TOK, HDIM), bf16)],
        1,
        place,
        in_hbm(cotangent),
        *sum(pairs, ())[1:],
        in_hbm(out_weight),
        in_hbm(attn_bwd),
        scratch=[pltpu.VMEM((4, GRAD_ROWS, HDIM), bf16)],
    )
    products = across(product, "x")
    summed = call(sum_kernel, pltpu.HBM((4 * TOK, HDIM), bf16), 0, products)
    grads = [grads[0]] + [along_x(grads[d], d) for d in range(1, 4)]
    parts = across(summed.reshape(8, HDIM, HDIM), "z")
    forward_out = call(forward_kernel, shape(4, GRAD_ROWS, HDIM), 1, place_x, own, halo)
    parts, forward_out, grads = lax.optimization_barrier((parts, forward_out, grads))
    chunks = call(last_sum_kernel, pltpu.HBM((8, HDIM, HDIM), bf16), 0, parts)
    gathered = across(chunks, "z").reshape(4 * TOK, HDIM)
    rest, grad_kv, ahead = call(
        backward_kernel,
        [
            pltpu.HBM((4, TOK + GRAD_ROWS, HDIM), bf16),
            pltpu.HBM((4, 2 * TOK, HDIM), f32),
            pltpu.HBM((HALO, 2 * TOK, HDIM), bf16),
        ],
        1,
        place_x,
        own,
        halo,
        *map(in_hbm, grads),
        forward_out,
        scratch=[pltpu.VMEM((4, GRAD_ROWS, HDIM), bf16)],
    )
    behind = next_row(ahead)
    gathered, ahead = lax.optimization_barrier((gathered, ahead))
    row_parts = [gathered] + [along_x(gathered, d) for d in range(1, 4)]
    crossed = across_y(row_parts[0], (1,))
    far_parts = [crossed, beside(crossed, 1)] + [across_y(part) for part in row_parts[1:]]
    behind, row_parts[3] = lax.optimization_barrier((behind, row_parts[3]))
    outs = call(
        finish_kernel,
        [pltpu.HBM((BACK_ROWS, HDIM), bf16)] * 4,
        1,
        place_x,
        in_hbm(rest),
        in_hbm(grad_kv),
        behind,
        scratch=[pltpu.VMEM((4, BACK_ROWS, HDIM), bf16)],
    )
    back = [outs[0]] + [along_x(outs[d], d) for d in range(1, 4)]
    block = (TOK, 4 * HDIM)
    return tuple(
        call(
            last_kernel,
            [
                shape(*block),
                shape(4, TOK, dtype=f32),
                shape(*block, dtype=f32),
                shape(*block, dtype=f32),
                shape(*block, dtype=f32),
                shape(2 * TOK, 16 * HDIM),
            ],
            1,
            place_x,
            in_hbm(back[0]),
            *back[1:],
            *row_parts,
            *far_parts,
            scratch=[
                pltpu.VMEM((3, *block), f32),
                pltpu.VMEM(block, bf16),
                pltpu.VMEM((4, TOK), f32),
                pltpu.VMEM((2 * TOK, 16 * HDIM), bf16),
                pltpu.VMEM((BACK_ROWS, HDIM), bf16),
                pltpu.SemaphoreType.DMA((14,)),
            ],
            raw_in=(1,),
            raw_out=True,
        )
    )


def solution(mesh):
    fine = Mesh(mesh.devices.reshape(2, 8, 4, 2, 2), ("yl", "z", "x", "yh", "core"))
    ctx, dp = ("yl", "z", "x"), ("yh", "core")
    in_specs = (
        P(ctx),
        P(ctx, dp),
        P(ctx, dp),
        P(ctx, dp),
        P(ctx),
        P(ctx, dp),
        P(ctx, dp),
        P(ctx, dp),
        P(ctx, dp),
        P(dp, ctx),
        P(ctx, dp),
        P(dp, None),
    )
    out_specs = (
        P(ctx, dp),
        P(dp, ctx),
        P(ctx, dp),
        P(ctx, dp),
        P(ctx, dp),
        P(dp, None),
    )
    return jax.shard_map(body, mesh=fine, in_specs=in_specs, out_specs=out_specs, check_vma=False)
```
